32 devices in a mesh: loop: 16 (over z, y, core), grp: 2 (over x).
Axes of the slice: x: 2, y: 2, z: 4, core: 2. Of those that a mesh axis runs over, the one named last changes fastest.
Arguments:
- jacobian: float32 [768, 16384], P('grp', 'loop'), may hold values from -0.21875 to 0.21875
Outputs:
- normal_matrix: float32 [16384, 16384], P(('loop', 'grp'))
The draws below stay inside these ranges and needn't reach their ends.
All inputs are finite; a program needn't handle non-finite values.
Results may differ from the reference program's by a relative error of at most 0.00007.
Values sent between devices are 32-bit elements; how exact they have to be, the bound alone decides.
No kernel may reach another device: no remote copies, remote signals or barrier semaphores. Data moves between devices by JAX's collectives and lax.ppermute only.
A program may use at most 192 MiB of HBM per device.

```python
import jax
import jax.numpy as jnp
from jax import lax

PARAMS = 16384
ROWS = 768


def steps_of(key, shape, cuts, low, top_value):
    level, own = 1.0, jax.random.fold_in(key, 6)
    for position, parts in cuts:
        heights = jnp.exp(jax.random.uniform(jax.random.fold_in(own, position), (parts,), jnp.float32, low / len(cuts), top_value / len(cuts)))
        level = level * jnp.repeat(heights, shape[position] // parts).reshape([-1 if axis == position else 1 for axis in range(len(shape))])
    return level


def scatter_about(stream_key, shape, scale, most, pieces=(), held_as=jnp.bfloat16):
    array = scale * jax.random.normal(stream_key, shape, jnp.float32)
    if pieces:
        array = array * steps_of(stream_key, shape, pieces, -0.22, 0.18)
    return jnp.clip(array, -most, most).astype(held_as)


def setup_inputs(seed: int = 0) -> dict:
    key_list = jax.random.split(jax.random.key(seed), 2)
    jacobian = scatter_about(key_list[0], (ROWS, PARAMS), ROWS ** -0.5, 0.21875, ((0, 2), (1, 16)), jnp.float32)
    return {"jacobian": jacobian}


damping = 0.1


def reference(jacobian):
    gram = jnp.dot(jacobian.T, jacobian, precision=lax.Precision.HIGHEST, preferred_element_type=jnp.float32)
    diag_index = jnp.arange(gram.shape[0], dtype=jnp.int32)
    return gram.at[diag_index, diag_index].multiply(1.0 + damping)
```

```python
import functools

import jax
import jax.numpy as jnp
from jax import lax
from jax.experimental import pallas as pl
from jax.experimental.pallas import tpu as pltpu
from jax.sharding import PartitionSpec as P

damping = 0.1
PASSES = 3
VMEM_BYTES = 40 * 1024 * 1024


def split_high_low(value):
    high = value.astype(jnp.bfloat16)
    low = (value - high.astype(jnp.float32)).astype(jnp.bfloat16)
    return high, low


def left_kernel(first_ref, second_ref, left_ref):
    depth = first_ref.shape[0]
    for place, ref in enumerate((first_ref, second_ref)):
        high, low = split_high_low(ref[...].T)
        for part, piece in enumerate((high, high, low)):
            left_ref[:, pl.ds(2 * depth * part + depth * place, depth)] = piece


def left_operand(first, second):
    depth, rows = first.shape
    return pl.pallas_call(
        left_kernel,
        out_shape=jax.ShapeDtypeStruct((rows, 2 * PASSES * depth), jnp.bfloat16),
        compiler_params=pltpu.CompilerParams(vmem_limit_bytes=VMEM_BYTES),
        name="left_operand",
    )(first, second)


def panel_kernel(sizes, tiles, diagonal, ids_ref, *refs):
    left_ref, out_ref, right_ref = refs[0], refs[-2], refs[-1]
    blocks = refs[1 : 1 + sum(map(sum, sizes))]
    step = pl.program_id(0)
    at = 0
    for index, counts in enumerate(sizes):
        groups = []
        for count in counts:
            groups.append(blocks[at : at + count])
            at += count

        @pl.when(step // tiles == index)
        def fill(groups=groups):
            depth = groups[0][0].shape[0]
            for place, group in enumerate(groups):
                value = functools.reduce(jnp.add, [ref[...] for ref in group])
                high, low = split_high_low(value)
                for part, piece in enumerate((high, low, high)):
                    right_ref[pl.ds(2 * depth * part + depth * place, depth), :] = piece

    product = jnp.dot(left_ref[...], right_ref[...], preferred_element_type=jnp.float32)
    if diagonal:
        width = product.shape[1]
        row_ids = lax.broadcasted_iota(jnp.int32, product.shape, 0) + ids_ref[len(sizes)]
        col_ids = lax.broadcasted_iota(jnp.int32, product.shape, 1) + (step % tiles) * width
        hit = (row_ids == col_ids) & (ids_ref[len(sizes) + 1 + step // tiles] == 1)
        product = jnp.where(hit, product * jnp.float32(1.0 + damping), product)
    out_ref[...] = product


def panels(out, left, columns, pairs, ids, diagonal=False):
    rows = left.shape[0]
    depth, width = pairs[0][0][0].shape
    tile = min(width, 512)
    tiles = width // tile
    sizes = tuple(tuple(len(half) for half in pair) for pair in pairs)
    operands, specs = [], []
    for index, pair in enumerate(pairs):
        for half in pair:
            for array in half:
                operands.append(array)
                specs.append(
                    pl.BlockSpec(
                        (depth, tile),
                        lambda t, ids, index=index: (0, jnp.clip(t - index * tiles, 0, tiles - 1)),
                    )
                )
    steps = len(pairs) * tiles
    in_specs = [pl.BlockSpec(left.shape, lambda t, ids: (0, 0))] + specs
    args = [ids, left] + operands
    aliases = {}
    if out is not None:
        aliases = {len(args): 0}
        args.append(out)
        in_specs.append(pl.BlockSpec(memory_space=pl.ANY))
    body = functools.partial(panel_kernel, sizes, tiles, diagonal)
    return pl.pallas_call(
        body,
        out_shape=jax.ShapeDtypeStruct((rows, columns), jnp.float32),
        grid_spec=pltpu.PrefetchScalarGridSpec(
            num_scalar_prefetch=1,
            grid=(steps,),
            in_specs=in_specs,
            out_specs=pl.BlockSpec((rows, tile), lambda t, ids: (0, ids[t // tiles] * tiles + t % tiles)),
            scratch_shapes=[pltpu.VMEM((left.shape[1], tile), jnp.bfloat16)],
        ),
        input_output_aliases=aliases,
        compiler_params=pltpu.CompilerParams(
            vmem_limit_bytes=VMEM_BYTES, dimension_semantics=("arbitrary",)
        ),
        cost_estimate=pl.CostEstimate(
            flops=2 * rows * left.shape[1] * width * len(pairs),
            bytes_accessed=4 * width * len(pairs) * (rows + 2 * depth),
            transcendentals=0,
        ),
        name="panels",
    )(*args)


def gathered(loop, grp, jacobian):
    rows_here = jacobian.shape[1] // grp
    me, side = lax.axis_index("loop"), lax.axis_index("grp")
    both = lax.all_gather(jacobian, "grp")
    everything = lax.all_gather(both, "loop")
    mine = lax.dynamic_slice_in_dim(both, side * rows_here, rows_here, axis=2)
    left = left_operand(mine[0], mine[1])
    out = None
    for panel in range(loop):
        ids = jnp.stack(
            [jnp.int32(panel), side * rows_here, (me == panel).astype(jnp.int32)]
        ).astype(jnp.int32)
        pair = ((everything[panel, 0],), (everything[panel, 1],))
        out = panels(out, left, jacobian.shape[1] * loop, [pair], ids, diagonal=True)
    return out


def rounds(loop, grp, jacobian):
    rows_here = jacobian.shape[1] // grp
    columns = jacobian.shape[1] * loop
    me, side = lax.axis_index("loop"), lax.axis_index("grp")
    z, y, core = me // 4, (me // 2) % 2, me % 2

    along_x = lambda v: lax.ppermute(v, "grp", [(0, 1), (1, 0)])
    along_y = lambda v: lax.ppermute(v, "loop", [(i, i ^ 2) for i in range(16)])
    pair_z = lambda v: lax.ppermute(v, "loop", [(i, i ^ 4) for i in range(16)])
    mid_z = lambda v: lax.ppermute(
        v, "loop", [(i, i + 4) for i in range(4, 8)] + [(i + 4, i) for i in range(4, 8)]
    )
    swap = lambda v: lax.ppermute(v, "loop", [(i, i ^ 1) for i in range(16)])

    c_self = jacobian
    x_self, y_self, c_mate, mid0 = along_x(c_self), along_y(c_self), pair_z(c_self), mid_z(c_self)

    d_self, y_mate, pair1, mid1 = along_x(y_self), along_y(c_mate), pair_z(mid0), mid_z(c_mate)
    c_near = pair1 + mid0

    x_near, y_near, d_mate = along_x(c_near), along_y(c_near), pair_z(d_self)

    x_mate, d_near, pair3, mid3 = along_x(c_mate), along_y(x_near), pair_z(mid1), mid_z(d_mate)
    c_far = pair3 + mid1

    x_far, y_far, pair4 = along_x(c_far), along_y(c_far), pair_z(mid3)

    mate_z = z ^ 1
    near_z = jnp.where(z < 2, 2, 1)
    far_z = jnp.where(z < 2, 3, 0)

    def ids_of(zz, yy, *more):
        base = zz * 4 + yy * 2
        return jnp.stack([base + core, base + 1 - core, *more]).astype(jnp.int32)

    def both(first, second):
        other = lambda half: tuple(swap(v) for v in half)
        return [(first, second), (other(first), other(second))]

    mine = lambda v: lax.dynamic_slice_in_dim(v, side * rows_here, rows_here, axis=1)
    left = left_operand(mine(c_self), mine(x_self))
    one, zero = jnp.int32(1), jnp.int32(0)
    ids = ids_of(z, y, side * rows_here, one, zero)
    out = panels(None, left, columns, both((c_self,), (x_self,)), ids, diagonal=True)
    out = panels(out, left, columns, both((y_self,), (d_self,)), ids_of(z, 1 - y))
    out = panels(out, left, columns, both((c_near,), (x_near,)), ids_of(near_z, y))
    out = panels(out, left, columns, both((y_mate,), (d_mate,)), ids_of(mate_z, 1 - y))
    out = panels(out, left, columns, both((c_mate,), (x_mate,)), ids_of(mate_z, y))
    out = panels(out, left, columns, both((y_near,), (d_near,)), ids_of(near_z, 1 - y))
    out = panels(out, left, columns, both((c_far,), (x_far,)), ids_of(far_z, y))
    out = panels(out, left, columns, both((y_far,), (pair4, mid3)), ids_of(far_z, 1 - y))
    return out


def solution(mesh):
    loop, grp = mesh.shape["loop"], mesh.shape["grp"]
    plan = rounds if (loop, grp) == (16, 2) else gathered
    return jax.shard_map(
        functools.partial(plan, loop, grp),
        mesh=mesh,
        in_specs=(P("grp", "loop"),),
        out_specs=P(("loop", "grp"), None),
        check_vma=False,
    )
```

```python
import functools

import jax
import jax.numpy as jnp
from jax import lax
from jax.experimental import pallas as pl
from jax.experimental.pallas import tpu as pltpu
from jax.sharding import PartitionSpec as P

damping = 0.1
PASSES = 3
VMEM_BYTES = 60 * 1024 * 1024
COST = 1024


def split_high_low(value):
    high = value.astype(jnp.bfloat16)
    low = (value - high.astype(jnp.float32)).astype(jnp.bfloat16)
    return high, low


def left_kernel(*refs):
    left_ref = refs[-1]
    depth, rows = refs[0].shape
    for block in range(len(refs) // 2):
        for place, ref in enumerate(refs[2 * block : 2 * block + 2]):
            high, low = split_high_low(ref[...].T)
            for part, piece in enumerate((high, high, low)):
                target = pl.ds(rows * block, rows), pl.ds(2 * depth * part + depth * place, depth)
                left_ref[target] = piece


def left_operand(*halves):
    depth, rows = halves[0].shape
    shape = rows * (len(halves) // 2), 2 * PASSES * depth
    return pl.pallas_call(
        left_kernel,
        out_shape=jax.ShapeDtypeStruct(shape, jnp.bfloat16),
        compiler_params=pltpu.CompilerParams(vmem_limit_bytes=VMEM_BYTES),
        cost_estimate=pl.CostEstimate(flops=COST, bytes_accessed=COST, transcendentals=0),
        name="left_operand",
    )(*halves)


def panel_kernel(sizes, diagonal, part, placed, tile, sends, ids_ref, *refs):
    count = sum(map(sum, sizes))
    left_hbm, blocks = refs[0], refs[1 : 1 + count]
    left_ref, held, done, stage_ref, left_sem, load_sem, store_sem, place_sem = refs[-8:]
    received_ref = refs[1 + count] if placed else None
    out_ref, send_ref = (refs[-10], refs[-9]) if sends else (refs[-9], None)
    width, rows = held.shape[-1], out_ref.shape[0]
    tiles, panel_count = width // tile, len(sizes)
    most = max(map(sum, sizes))
    left_copy = pltpu.make_async_copy(left_hbm.at[pl.ds(0, left_ref.shape[0])], left_ref, left_sem)
    loads, at = [], 0
    for index, counts in enumerate(sizes):
        loads.append([])
        for place in range(sum(counts)):
            here = index % 2, place
            loads[index].append(pltpu.make_async_copy(blocks[at], held.at[here], load_sem.at[here]))
            at += 1
    fetches, puts = [], []
    if placed:
        first, whole = placed
        for index in range(received_ref.shape[0]):
            column = pl.multiple_of(ids_ref[panel_count + index] * whole + first, 128)
            target = out_ref.at[:, pl.ds(column, received_ref.shape[-1])]
            stage = stage_ref.at[index]
            fetches.append(pltpu.make_async_copy(received_ref.at[index], stage, place_sem.at[index, 0]))
            puts.append(pltpu.make_async_copy(stage, target, place_sem.at[index, 1]))

    def stores(turn):
        first, whole = part
        index, column = turn // tiles, pl.multiple_of(lax.rem(turn, tiles) * tile, 128)
        slot = lax.rem(turn, 2)
        place = pl.multiple_of(ids_ref[index] * whole + first + column, 128)
        copies = [(done.at[slot, pl.ds(0, rows)], out_ref.at[:, pl.ds(place, tile)], store_sem.at[slot, 0])]
        if sends:
            target = send_ref.at[index, :, pl.ds(column, tile)]
            copies.append((done.at[slot, pl.ds(rows, rows)], target, store_sem.at[slot, 1]))
        return [pltpu.make_async_copy(*copy) for copy in copies]

    for copy in loads[0] + [left_copy] + (loads[1] if panel_count > 1 else []) + fetches:
        copy.start()
    left_copy.wait()
    turns = panel_count * tiles

    def turn_body(turn, carry):
        index, column = turn // tiles, pl.multiple_of(lax.rem(turn, tiles) * tile, 128)
        slot = lax.rem(index, 2)
        for here, copies in enumerate(loads):

            @pl.when(turn == here * tiles)
            def arrive(copies=copies):
                for copy in copies:
                    copy.wait()

        @pl.when(turn >= 2)
        def free():
            for copy in stores(turn - 2):
                copy.wait()

        @pl.when(turn == min(1, turns - 1))
        def put():
            for fetch, put in zip(fetches, puts):
                fetch.wait()
                put.start()

        block = [held[slot, k, :, pl.ds(column, tile)] for k in range(most)]
        if most > 2:
            extra = functools.reduce(jnp.logical_or, [index == i for i, n in enumerate(sizes) if sum(n) > 2])
            block[1] = block[1] + jnp.where(extra, block[2], 0.0)
        halves = [split_high_low(value) for value in block[:2]]
        high, low = (jnp.concatenate(pieces, axis=0) for pieces in zip(*halves))
        right = jnp.concatenate([high, low, high], axis=0)
        product = jnp.dot(left_ref[...], right, preferred_element_type=jnp.float32)
        if diagonal is not None:
            row_ids = lax.broadcasted_iota(jnp.int32, product.shape, 0) + ids_ref[ids_ref.shape[0] - 1]
            col_ids = lax.broadcasted_iota(jnp.int32, product.shape, 1) + column
            own = lax.broadcasted_iota(jnp.int32, product.shape, 0) < rows
            hit = (row_ids == col_ids) & own & (index == diagonal)
            product = jnp.where(hit, product * jnp.float32(1.0 + damping), product)
        done[lax.rem(turn, 2)] = product
        for copy in stores(turn):
            copy.start()
        for here in range(panel_count - 2):

            @pl.when(turn == here * tiles + tiles - 1)
            def fetch(copies=loads[here + 2]):
                for copy in copies:
                    copy.start()

        return carry

    lax.fori_loop(0, turns, turn_body, 0)
    for turn in range(max(0, turns - 2), turns):
        for copy in stores(turn):
            copy.wait()
    for copy in puts:
        copy.wait()


def panels(out, left, rows, columns, pairs, ids, received=None, placed=None, diagonal=None, part=None, sends=False, tile=None):
    depth, width = pairs[0][0][0].shape
    sizes = tuple(tuple(len(half) for half in pair) for pair in pairs)
    args = [ids, left] + [array for pair in pairs for half in pair for array in half]
    if received is not None:
        args.append(received)
    aliases = {}
    if out is not None:
        aliases = {len(args): 0}
        args.append(out)
    anywhere = pl.BlockSpec(memory_space=pl.ANY)
    most = max(map(sum, sizes))
    tile = tile or min(256, width)
    height = 2 * rows if sends else rows
    shapes = [jax.ShapeDtypeStruct((rows, columns), jnp.float32)]
    if sends:
        shapes.append(jax.ShapeDtypeStruct((len(pairs), rows, width), jnp.float32))
    outs = pl.pallas_call(
        functools.partial(panel_kernel, sizes, diagonal, part or (0, width), placed, tile, sends),
        out_shape=shapes,
        in_specs=[pl.BlockSpec(memory_space=pltpu.SMEM)] + [anywhere] * (len(args) - 1),
        out_specs=[anywhere] * len(shapes),
        scratch_shapes=[
            pltpu.VMEM((height, left.shape[1]), left.dtype),
            pltpu.VMEM((2, most, depth, width), jnp.float32),
            pltpu.VMEM((2, height, tile), jnp.float32),
            pltpu.VMEM(received.shape if placed else (8, 128), jnp.float32),
            pltpu.SemaphoreType.DMA,
            pltpu.SemaphoreType.DMA((2, most)),
            pltpu.SemaphoreType.DMA((2, 2)),
            pltpu.SemaphoreType.DMA((received.shape[0] if placed else 1, 2)),
        ],
        input_output_aliases=aliases,
        compiler_params=pltpu.CompilerParams(vmem_limit_bytes=VMEM_BYTES),
        cost_estimate=pl.CostEstimate(
            flops=20 * height * left.shape[1] * width * len(pairs),
            bytes_accessed=4 * width * len(pairs) * (height + 2 * depth),
            transcendentals=0,
        ),
        name="panels",
    )(*args)
    return outs if sends else outs[0]


def place_kernel(placed, ids_ref, received_ref, _, out_ref, stage_ref, place_sem):
    first, whole = placed
    fetches, puts = [], []
    for index in range(received_ref.shape[0]):
        column = pl.multiple_of(ids_ref[index] * whole + first, 128)
        target = out_ref.at[:, pl.ds(column, received_ref.shape[-1])]
        stage = stage_ref.at[index]
        fetches.append(pltpu.make_async_copy(received_ref.at[index], stage, place_sem.at[index, 0]))
        puts.append(pltpu.make_async_copy(stage, target, place_sem.at[index, 1]))
    for fetch in fetches:
        fetch.start()
    for fetch, put in zip(fetches, puts):
        fetch.wait()
        put.start()
    for put in puts:
        put.wait()


def place(out, received, ids, placed):
    anywhere = pl.BlockSpec(memory_space=pl.ANY)
    return pl.pallas_call(
        functools.partial(place_kernel, placed),
        out_shape=jax.ShapeDtypeStruct(out.shape, out.dtype),
        in_specs=[pl.BlockSpec(memory_space=pltpu.SMEM), anywhere, anywhere],
        out_specs=anywhere,
        scratch_shapes=[
            pltpu.VMEM(received.shape, received.dtype),
            pltpu.SemaphoreType.DMA((received.shape[0], 2)),
        ],
        input_output_aliases={2: 0},
        compiler_params=pltpu.CompilerParams(vmem_limit_bytes=VMEM_BYTES),
        cost_estimate=pl.CostEstimate(flops=0, bytes_accessed=8 * received.size, transcendentals=0),
        name="place",
    )(ids, received, out)


def gathered(loop, grp, jacobian):
    rows_here = jacobian.shape[1] // grp
    me, side = lax.axis_index("loop"), lax.axis_index("grp")
    both = lax.all_gather(jacobian, "grp")
    everything = lax.all_gather(both, "loop")
    mine = lax.dynamic_slice_in_dim(both, side * rows_here, rows_here, axis=2)
    left = left_operand(mine[0], mine[1])
    out = None
    for turn in range(loop):
        panel = (me + turn) % loop
        pair = tuple((lax.dynamic_index_in_dim(everything, panel, keepdims=False)[g],) for g in range(2))
        ids = jnp.stack([panel, side * rows_here]).astype(jnp.int32)
        out = panels(out, left, rows_here, jacobian.shape[1] * loop, [pair], ids, diagonal=None if turn else 0)
    return out


def rounds(loop, grp, jacobian):
    width = jacobian.shape[1]
    rows_here, columns = width // grp, width * loop
    me, side = lax.axis_index("loop"), lax.axis_index("grp")
    z, y, core = me // 4, (me // 2) % 2, me % 2

    along_x = lambda v: lax.ppermute(v, "grp", [(0, 1), (1, 0)])
    along_y = lambda v: lax.ppermute(v, "loop", [(i, i ^ 2) for i in range(16)])
    pair_z = lambda v: lax.ppermute(v, "loop", [(i, i ^ 4) for i in range(16)])
    mid_z = lambda v: lax.ppermute(
        v, "loop", [(i, i + 4) for i in range(4, 8)] + [(i + 4, i) for i in range(4, 8)]
    )
    swap = lambda v: lax.ppermute(v, "loop", [(i, i ^ 1) for i in range(16)])
    together = lax.optimization_barrier

    mate_z = z ^ 1
    near_z = jnp.where(z < 2, 2, 1)
    far_z = jnp.where(z < 2, 3, 0)
    shift = side * rows_here
    places = [(z, y), (z, 1 - y), (near_z, y), (mate_z, 1 - y), (mate_z, y), (near_z, 1 - y), (far_z, y), (far_z, 1 - y)]
    own = [zz * 4 + yy * 2 + core for zz, yy in places]
    other = [zz * 4 + yy * 2 + 1 - core for zz, yy in places]
    number = lambda *numbers: jnp.stack(numbers).astype(jnp.int32)
    ids = tuple(number(*n) for n in (own[:1] + [shift], own[1:2], own[2:4], own[4:6], own[6:], other[6:] + other[4:6]))
    put = tuple(number(*n) for n in (other[:1], other[1:2], other[2:4]))
    step = lambda out, left, turn, pairs, **kw: panels(out, left, rows_here, columns, pairs, ids[turn], **kw)
    whole = 0, width

    c = jacobian
    x_self, y_self, c_mate, mid0 = along_x(c), along_y(c), pair_z(c), mid_z(c)
    own_columns = lambda v: lax.dynamic_slice_in_dim(v, shift, rows_here, axis=1)
    own_c = own_columns(c)
    own_c_o = swap(own_c)
    x_self, y_self, c_mate, mid0, own_c, own_c_o, ids, put = together(
        (x_self, y_self, c_mate, mid0, own_c, own_c_o, ids, put)
    )

    d_self, y_mate, pair1, mid1 = along_x(y_self), along_y(c_mate), pair_z(mid0), mid_z(c_mate)
    own_x = own_columns(x_self)
    left = left_operand(own_c, own_x, own_c_o, swap(own_x))
    out, send1 = step(None, left, 0, [((c,), (x_self,))], diagonal=0, sends=True)
    d_self, y_mate, pair1, mid1, out = together((d_self, y_mate, pair1, mid1, out))

    d_mate = pair_z(d_self)
    c_near = pair1 + mid0
    x_near, y_near = along_x(c_near), along_y(c_near)
    out, send2 = step(out, left, 1, [((y_self,), (d_self,))], sends=True)
    out = place(out, swap(send1), put[0], whole)
    d_mate, x_near, y_near, c_near, c_mate, mid1, out = together(
        (d_mate, x_near, y_near, c_near, c_mate, mid1, out)
    )

    x_mate, d_near, pair3, mid3 = along_x(c_mate), along_y(x_near), pair_z(mid1), mid_z(d_mate)
    out, send3 = step(out, left, 2, [((c_near,), (x_near,)), ((y_mate,), (d_mate,))], sends=True)
    out = place(out, swap(send2), put[1], whole)
    x_mate, d_near, pair3, mid1, mid3, out = together((x_mate, d_near, pair3, mid1, mid3, out))

    d_far = pair_z(mid3)
    c_far = pair3 + mid1
    x_far, y_far = along_x(c_far), along_y(c_far)
    out, send4 = step(out, left, 3, [((c_mate,), (x_mate,)), ((y_near,), (d_near,))], sends=True)
    out = place(out, swap(send3), put[2], whole)
    c_far_o = swap(c_far)
    x_far, y_far, d_far, c_far, c_far_o, mid3, out = together((x_far, y_far, d_far, c_far, c_far_o, mid3, out))

    out = step(out, left, 4, [((c_far,), (x_far,)), ((y_far,), (d_far, mid3))])
    pairs = [((c_far_o,), (swap(x_far),)), ((swap(y_far),), (swap(d_far + mid3),))]
    return step(out, left, 5, pairs, received=swap(send4), placed=whole)


def solution(mesh):
    loop, grp = mesh.shape["loop"], mesh.shape["grp"]
    plan = rounds if (loop, grp) == (16, 2) else gathered
    return jax.shard_map(
        functools.partial(plan, loop, grp),
        mesh=mesh,
        in_specs=(P("grp", "loop"),),
        out_specs=P(("loop", "grp"), None),
        check_vma=False,
    )
```

```python
import functools

import jax
import jax.numpy as jnp
from jax import lax
from jax.experimental import pallas as pl
from jax.experimental.pallas import tpu as pltpu
from jax.sharding import PartitionSpec as P

damping = 0.1
VMEM_BYTES = 60 * 1024 * 1024
COST = 1024


def split_high_low(value):
    high = value.astype(jnp.bfloat16)
    low = (value - high.astype(jnp.float32)).astype(jnp.bfloat16)
    return high, low


def left_kernel(*refs):
    left_ref = refs[-1]
    depth, rows = refs[0].shape
    for block in range(len(refs) // 2):
        for place, ref in enumerate(refs[2 * block : 2 * block + 2]):
            high, low = split_high_low(ref[...].T)
            for part, piece in enumerate((high, low)):
                target = pl.ds(rows * block, rows), pl.ds(2 * depth * part + depth * place, depth)
                left_ref[target] = piece


def left_operand(*halves):
    depth, rows = halves[0].shape
    shape = rows * (len(halves) // 2), 4 * depth
    return pl.pallas_call(
        left_kernel,
        out_shape=jax.ShapeDtypeStruct(shape, jnp.bfloat16),
        compiler_params=pltpu.CompilerParams(vmem_limit_bytes=VMEM_BYTES),
        cost_estimate=pl.CostEstimate(flops=COST, bytes_accessed=COST, transcendentals=0),
        name="left_operand",
    )(*halves)


def panel_kernel(sizes, diagonal, part, placed, tile, sends, ids_ref, *refs):
    count = sum(map(sum, sizes))
    left_ref, blocks = refs[0], refs[1 : 1 + count]
    held, done, stage_ref, load_sem, store_sem, place_sem = refs[-6:]
    received_ref = refs[1 + count] if placed else None
    out_ref, send_ref = (refs[-8], refs[-7]) if sends else (refs[-7], None)
    width, rows = held.shape[-1], out_ref.shape[0]
    tiles, panel_count = width // tile, len(sizes)
    most = max(map(sum, sizes))
    height, depth = done.shape[1], left_ref.shape[1] // 2
    left = [left_ref.at[pl.ds(0, height), pl.ds(k * depth, depth)] for k in range(2)]
    loads, at = [], 0
    for index, counts in enumerate(sizes):
        loads.append([])
        for place in range(sum(counts)):
            here = index % 2, place
            loads[index].append(pltpu.make_async_copy(blocks[at], held.at[here], load_sem.at[here]))
            at += 1
    fetches, puts = [], []
    if placed:
        first, whole = placed
        for index in range(received_ref.shape[0]):
            column = pl.multiple_of(ids_ref[panel_count + index] * whole + first, 128)
            target = out_ref.at[:, pl.ds(column, received_ref.shape[-1])]
            stage = stage_ref.at[index]
            fetches.append(pltpu.make_async_copy(received_ref.at[index], stage, place_sem.at[index, 0]))
            puts.append(pltpu.make_async_copy(stage, target, place_sem.at[index, 1]))

    def stores(turn):
        first, whole = part
        index, column = turn // tiles, pl.multiple_of(lax.rem(turn, tiles) * tile, 128)
        slot = lax.rem(turn, 2)
        place = pl.multiple_of(ids_ref[index] * whole + first + column, 128)
        copies = [(done.at[slot, pl.ds(0, rows)], out_ref.at[:, pl.ds(place, tile)], store_sem.at[slot, 0])]
        if sends:
            target = send_ref.at[index, :, pl.ds(column, tile)]
            copies.append((done.at[slot, pl.ds(rows, rows)], target, store_sem.at[slot, 1]))
        return [pltpu.make_async_copy(*copy) for copy in copies]

    for copy in loads[0] + (loads[1] if panel_count > 1 else []) + fetches:
        copy.start()
    turns = panel_count * tiles

    def turn_body(turn, carry):
        index, column = turn // tiles, pl.multiple_of(lax.rem(turn, tiles) * tile, 128)
        slot = lax.rem(index, 2)
        for here, copies in enumerate(loads):

            @pl.when(turn == here * tiles)
            def arrive(copies=copies):
                for copy in copies:
                    copy.wait()

        @pl.when(turn >= 2)
        def free():
            for copy in stores(turn - 2):
                copy.wait()

        @pl.when(turn == min(1, turns - 1))
        def put():
            for fetch, put in zip(fetches, puts):
                fetch.wait()
                put.start()

        block = [held[slot, k, :, pl.ds(column, tile)] for k in range(most)]
        if most > 2:
            extra = functools.reduce(jnp.logical_or, [index == i for i, n in enumerate(sizes) if sum(n) > 2])
            block[1] = block[1] + jnp.where(extra, block[2], 0.0)
        halves = [split_high_low(value) for value in block[:2]]
        high, low = (jnp.concatenate(pieces, axis=0) for pieces in zip(*halves))
        dot = functools.partial(jnp.dot, preferred_element_type=jnp.float32)
        product = dot(left[0][...], high) + dot(left[0][...], low) + dot(left[1][...], high)
        if diagonal is not None:
            row_ids = lax.broadcasted_iota(jnp.int32, product.shape, 0) + ids_ref[ids_ref.shape[0] - 1]
            col_ids = lax.broadcasted_iota(jnp.int32, product.shape, 1) + column
            own = lax.broadcasted_iota(jnp.int32, product.shape, 0) < rows
            hit = (row_ids == col_ids) & own & (index == diagonal)
            product = jnp.where(hit, product * jnp.float32(1.0 + damping), product)
        done[lax.rem(turn, 2)] = product
        for copy in stores(turn):
            copy.start()
        for here in range(panel_count - 2):

            @pl.when(turn == here * tiles + tiles - 1)
            def fetch(copies=loads[here + 2]):
                for copy in copies:
                    copy.start()

        return carry

    lax.fori_loop(0, turns, turn_body, 0)
    for turn in range(max(0, turns - 2), turns):
        for copy in stores(turn):
            copy.wait()
    for copy in puts:
        copy.wait()


def panels(out, left, rows, columns, pairs, ids, received=None, placed=None, diagonal=None, part=None, sends=False, tile=None):
    depth, width = pairs[0][0][0].shape
    sizes = tuple(tuple(len(half) for half in pair) for pair in pairs)
    args = [ids, left] + [array for pair in pairs for half in pair for array in half]
    if received is not None:
        args.append(received)
    aliases = {}
    if out is not None:
        aliases = {len(args): 0}
        args.append(out)
    anywhere = pl.BlockSpec(memory_space=pl.ANY)
    most = max(map(sum, sizes))
    tile = tile or min(256 if sends else 512, width)
    height = 2 * rows if sends else rows
    shapes = [jax.ShapeDtypeStruct((rows, columns), jnp.float32)]
    if sends:
        shapes.append(jax.ShapeDtypeStruct((len(pairs), rows, width), jnp.float32))
    outs = pl.pallas_call(
        functools.partial(panel_kernel, sizes, diagonal, part or (0, width), placed, tile, sends),
        out_shape=shapes,
        in_specs=[pl.BlockSpec(memory_space=pltpu.SMEM), pl.BlockSpec(memory_space=pltpu.VMEM)]
        + [anywhere] * (len(args) - 2),
        out_specs=[anywhere] * len(shapes),
        scratch_shapes=[
            pltpu.VMEM((2, most, depth, width), jnp.float32),
            pltpu.VMEM((2, height, tile), jnp.float32),
            pltpu.VMEM(received.shape if placed else (8, 128), jnp.float32),
            pltpu.SemaphoreType.DMA((2, most)),
            pltpu.SemaphoreType.DMA((2, 2)),
            pltpu.SemaphoreType.DMA((received.shape[0] if placed else 1, 2)),
        ],
        input_output_aliases=aliases,
        compiler_params=pltpu.CompilerParams(vmem_limit_bytes=VMEM_BYTES),
        cost_estimate=pl.CostEstimate(
            flops=30 * height * left.shape[1] * width * len(pairs),
            bytes_accessed=4 * width * len(pairs) * (height + 2 * depth),
            transcendentals=0,
        ),
        name="panels",
    )(*args)
    return outs if sends else outs[0]


def place_kernel(placed, ids_ref, received_ref, _, out_ref, stage_ref, place_sem):
    first, whole = placed
    fetches, puts = [], []
    for index in range(received_ref.shape[0]):
        column = pl.multiple_of(ids_ref[index] * whole + first, 128)
        target = out_ref.at[:, pl.ds(column, received_ref.shape[-1])]
        stage = stage_ref.at[index]
        fetches.append(pltpu.make_async_copy(received_ref.at[index], stage, place_sem.at[index, 0]))
        puts.append(pltpu.make_async_copy(stage, target, place_sem.at[index, 1]))
    for fetch in fetches:
        fetch.start()
    for fetch, put in zip(fetches, puts):
        fetch.wait()
        put.start()
    for put in puts:
        put.wait()


def place(out, received, ids, placed):
    anywhere = pl.BlockSpec(memory_space=pl.ANY)
    return pl.pallas_call(
        functools.partial(place_kernel, placed),
        out_shape=jax.ShapeDtypeStruct(out.shape, out.dtype),
        in_specs=[pl.BlockSpec(memory_space=pltpu.SMEM), anywhere, anywhere],
        out_specs=anywhere,
        scratch_shapes=[
            pltpu.VMEM(received.shape, received.dtype),
            pltpu.SemaphoreType.DMA((received.shape[0], 2)),
        ],
        input_output_aliases={2: 0},
        compiler_params=pltpu.CompilerParams(vmem_limit_bytes=VMEM_BYTES),
        cost_estimate=pl.CostEstimate(flops=0, bytes_accessed=8 * received.size, transcendentals=0),
        name="place",
    )(ids, received, out)


def choose_kernel(flag_ref, first_ref, second_ref, out_ref, sems):
    rows = out_ref.shape[0] // sems.shape[0]
    pieces = [pl.ds(k * rows, rows) for k in range(sems.shape[0])]
    for value, ref in ((1, first_ref), (0, second_ref)):

        @pl.when(flag_ref[0] == value)
        def copy(ref=ref):
            for k, piece in enumerate(pieces):
                pltpu.make_async_copy(ref.at[piece], out_ref.at[piece], sems.at[k]).start()

    for k, piece in enumerate(pieces):
        pltpu.make_async_copy(first_ref.at[piece], out_ref.at[piece], sems.at[k]).wait()


def choose(flag, first, second):
    anywhere = pl.BlockSpec(memory_space=pl.ANY)
    return pl.pallas_call(
        choose_kernel,
        out_shape=jax.ShapeDtypeStruct(first.shape, first.dtype),
        in_specs=[pl.BlockSpec(memory_space=pltpu.SMEM), anywhere, anywhere],
        out_specs=pl.BlockSpec(memory_space=pltpu.VMEM),
        scratch_shapes=[pltpu.SemaphoreType.DMA((4,))],
        cost_estimate=pl.CostEstimate(flops=0, bytes_accessed=4 * first.size, transcendentals=0),
        name="choose",
    )(flag, first, second)


def gathered(loop, grp, jacobian):
    rows_here = jacobian.shape[1] // grp
    me, side = lax.axis_index("loop"), lax.axis_index("grp")
    both = lax.all_gather(jacobian, "grp")
    everything = lax.all_gather(both, "loop")
    mine = lax.dynamic_slice_in_dim(both, side * rows_here, rows_here, axis=2)
    left = left_operand(mine[0], mine[1])
    out = None
    for turn in range(loop):
        panel = (me + turn) % loop
        pair = tuple((lax.dynamic_index_in_dim(everything, panel, keepdims=False)[g],) for g in range(2))
        ids = jnp.stack([panel, side * rows_here]).astype(jnp.int32)
        out = panels(out, left, rows_here, jacobian.shape[1] * loop, [pair], ids, diagonal=None if turn else 0)
    return out


def rounds(loop, grp, jacobian):
    width = jacobian.shape[1]
    rows_here, columns = width // grp, width * loop
    me, side = lax.axis_index("loop"), lax.axis_index("grp")
    z, y, core = me // 4, (me // 2) % 2, me % 2

    along_x = lambda v: lax.ppermute(v, "grp", [(0, 1), (1, 0)])
    along_y = lambda v: lax.ppermute(v, "loop", [(i, i ^ 2) for i in range(16)])
    pair_z = lambda v: lax.ppermute(v, "loop", [(i, i ^ 4) for i in range(16)])
    mid_z = lambda v: lax.ppermute(
        v, "loop", [(i, i + 4) for i in range(4, 8)] + [(i + 4, i) for i in range(4, 8)]
    )
    swap = lambda v: lax.ppermute(v, "loop", [(i, i ^ 1) for i in range(16)])
    together = lax.optimization_barrier
    after = lambda value, *first: together((value, first))[0]

    mate_z = z ^ 1
    near_z = jnp.where(z < 2, 2, 1)
    far_z = jnp.where(z < 2, 3, 0)
    shift = side * rows_here
    places = [(z, y), (z, 1 - y), (near_z, y), (mate_z, 1 - y), (mate_z, y), (near_z, 1 - y), (far_z, y), (far_z, 1 - y)]
    own = [zz * 4 + yy * 2 + core for zz, yy in places]
    other = [zz * 4 + yy * 2 + 1 - core for zz, yy in places]
    number = lambda *numbers: jnp.stack(numbers).astype(jnp.int32)
    ids = tuple(number(*n) for n in (own[:2] + [shift], own[2:4], own[4:6], own[6:], other[6:] + other[4:6]))
    put = tuple(number(*n) for n in (other[:2], other[2:4]))
    outer = number((z == 0) | (z == 3))
    step = lambda out, left, turn, pairs, **kw: panels(out, left, rows_here, columns, pairs, ids[turn], **kw)
    whole = 0, width

    c = jacobian
    x_self, mid0, c_mate, y_self = along_x(c), mid_z(c), pair_z(c), along_y(c)
    own_columns = lambda v: lax.dynamic_slice_in_dim(v, shift, rows_here, axis=1)
    own_c = own_columns(c)
    own_c_o = swap(own_c)
    mid0, own_c, own_c_o, ids, put, outer = together((mid0, own_c, own_c_o, ids, put, outer))

    pair1 = pair_z(after(mid0, c_mate))
    mid1 = mid_z(c_mate)
    y_mate = along_y(after(c_mate, y_self))
    d_self = along_x(after(y_self, x_self))
    own_x = own_columns(x_self)
    left = left_operand(own_c, own_x, own_c_o, swap(own_x))

    c_near = choose(outer, after(pair1, left), mid0)
    d_mate = pair_z(after(d_self, pair1, left))
    y_near = along_y(after(c_near, y_mate))
    x_near = along_x(after(c_near, d_self))
    out, send2 = step(None, left, 0, [((c,), (x_self,)), ((y_self,), (d_self,))], diagonal=0, sends=True)

    pair3 = pair_z(after(mid1, d_mate, out))
    mid3 = mid_z(after(d_mate, out))
    d_near = along_y(after(x_near, y_near))
    x_mate = along_x(after(c_mate, x_near))
    out, send3 = step(out, left, 1, [((c_near,), (x_near,)), ((y_mate,), (d_mate,))], sends=True)
    out = place(out, swap(send2), put[0], whole)

    c_far = choose(outer, after(pair3, out), mid1)
    x_far = along_x(after(c_far, x_mate))
    d_far = pair_z(after(mid3, pair3, out))
    y_far = along_y(after(c_far, d_near))
    out, send4 = step(out, left, 2, [((c_mate,), (x_mate,)), ((y_near,), (d_near,))], sends=True)
    out = place(out, swap(send3), put[1], whole)
    c_far_o = swap(c_far)
    x_far, y_far, d_far, c_far, c_far_o, mid3, out = together((x_far, y_far, d_far, c_far, c_far_o, mid3, out))

    out = step(out, left, 3, [((c_far,), (x_far,)), ((y_far,), (d_far, mid3))])
    pairs = [((c_far_o,), (swap(x_far),)), ((swap(y_far),), (swap(d_far), swap(mid3)))]
    return step(out, left, 4, pairs, received=swap(send4), placed=whole)


def solution(mesh):
    loop, grp = mesh.shape["loop"], mesh.shape["grp"]
    plan = rounds if (loop, grp) == (16, 2) else gathered
    return jax.shard_map(
        functools.partial(plan, loop, grp),
        mesh=mesh,
        in_specs=(P("grp", "loop"),),
        out_specs=P(("loop", "grp"), None),
        check_vma=False,
    )
```

```python
import functools

import jax
import jax.numpy as jnp
from jax import lax
from jax.experimental import pallas as pl
from jax.experimental.pallas import tpu as pltpu
from jax.sharding import PartitionSpec as P

damping = 0.1
VMEM_BYTES = 63 * 1024 * 1024 + 512 * 1024
COST = 1024


def split_high_low(value):
    high = value.astype(jnp.bfloat16)
    low = (value - high.astype(jnp.float32)).astype(jnp.bfloat16)
    return high, low


def left_kernel(*refs):
    left_ref = refs[-1]
    depth, rows = refs[0].shape
    for block in range(len(refs) // 2):
        for place, ref in enumerate(refs[2 * block : 2 * block + 2]):
            high, low = split_high_low(ref[...].T)
            for part, piece in enumerate((high, low)):
                target = pl.ds(rows * block, rows), pl.ds(2 * depth * part + depth * place, depth)
                left_ref[target] = piece


def left_operand(*halves):
    depth, rows = halves[0].shape
    shape = rows * (len(halves) // 2), 4 * depth
    return pl.pallas_call(
        left_kernel,
        out_shape=jax.ShapeDtypeStruct(shape, jnp.bfloat16),
        compiler_params=pltpu.CompilerParams(vmem_limit_bytes=VMEM_BYTES),
        cost_estimate=pl.CostEstimate(flops=COST, bytes_accessed=COST, transcendentals=0),
        name="left_operand",
    )(*halves)


def panel_kernel(sizes, diagonal, part, placed, width, tile, sends, ids_ref, left_hbm, *refs):
    count = sum(map(sum, sizes))
    blocks, received = refs[:count], refs[count : count + len(placed)]
    left_ref, held, done, left_sem, load_sem, store_sem, place_sem = refs[-7 - len(placed) : len(refs) - len(placed)]
    stages = refs[len(refs) - len(placed) :]
    out_ref, send_ref = refs[-9 - len(placed) : -7 - len(placed)] if sends else (refs[-8 - len(placed)], None)
    rows, (first, whole) = out_ref.shape[0], part
    tiles, panel_count = width // tile, len(sizes)
    turns = panel_count * tiles
    most = max(map(sum, sizes))
    height, depth = done.shape[1], left_ref.shape[1] // 2
    left = [left_ref.at[:, pl.ds(k * depth, depth)] for k in range(2)]
    left_copy = pltpu.make_async_copy(left_hbm.at[pl.ds(0, height)], left_ref, left_sem)

    loads, at = [], 0
    for index, counts in enumerate(sizes):
        loads.append([[] for _ in range(tiles)])
        for place in range(sum(counts)):
            skip = first if blocks[at].shape[1] > width else 0
            for t in range(tiles):
                source = blocks[at].at[:, pl.ds(skip + t * tile, tile)]
                target = held.at[index % 2, place, :, pl.ds(t * tile, tile)]
                loads[index][t].append(pltpu.make_async_copy(source, target, load_sem.at[index % 2, place, t]))
            at += 1
    fetches, puts, at = [], [], panel_count
    for number, (from_ref, stage, (begin, size)) in enumerate(zip(received, stages, placed)):
        for index in range(from_ref.shape[0]):
            column = pl.multiple_of(ids_ref[at] * size + begin, 128)
            target = out_ref.at[:, pl.ds(column, from_ref.shape[-1])]
            fetches.append(pltpu.make_async_copy(from_ref.at[index], stage.at[index], place_sem.at[number, index, 0]))
            puts.append(pltpu.make_async_copy(stage.at[index], target, place_sem.at[number, index, 1]))
            at += 1

    def stores(turn):
        index, column = turn // tiles, pl.multiple_of(lax.rem(turn, tiles) * tile, 128)
        slot = lax.rem(turn, 2)
        place = pl.multiple_of(ids_ref[index] * whole + first + column, 128)
        copies = [(done.at[slot, pl.ds(0, rows)], out_ref.at[:, pl.ds(place, tile)], store_sem.at[slot, 0])]
        if sends:
            target = send_ref.at[index, :, pl.ds(column, tile)]
            copies.append((done.at[slot, pl.ds(rows, rows)], target, store_sem.at[slot, 1]))
        return [pltpu.make_async_copy(*copy) for copy in copies]

    def start(copies):
        for copy in copies:
            copy.start()

    def wait(copies):
        for copy in copies:
            copy.wait()

    start(loads[0][0] + [left_copy])
    for copies in loads[0][1:]:
        start(copies)
    left_copy.wait()

    def turn_body(turn, carry):
        index, column = turn // tiles, pl.multiple_of(lax.rem(turn, tiles) * tile, 128)
        slot = lax.rem(index, 2)
        for here in range(turns):

            @pl.when(turn == here)
            def arrive(here=here):
                wait(loads[here // tiles][here % tiles])
                if here == 0:
                    for copies in loads[1] if panel_count > 1 else []:
                        start(copies)
                    start(fetches)

        @pl.when(turn >= 2)
        def free():
            wait(stores(turn - 2))

        @pl.when(turn == turns // 2)
        def put():
            wait(fetches)
            start(puts)

        block = [held[slot, k, :, pl.ds(column, tile)] for k in range(most)]
        if most > 2:
            extra = functools.reduce(jnp.logical_or, [index == i for i, n in enumerate(sizes) if sum(n) > 2])
            block[1] = block[1] + jnp.where(extra, block[2], 0.0)
        halves = [split_high_low(value) for value in block[:2]]
        high, low = (jnp.concatenate(pieces, axis=0) for pieces in zip(*halves))
        dot = functools.partial(jnp.dot, preferred_element_type=jnp.float32)
        product = dot(left[0][...], high) + dot(left[0][...], low) + dot(left[1][...], high)
        if diagonal is not None:
            row_ids = lax.broadcasted_iota(jnp.int32, product.shape, 0) + ids_ref[ids_ref.shape[0] - 1]
            col_ids = lax.broadcasted_iota(jnp.int32, product.shape, 1) + column
            own = lax.broadcasted_iota(jnp.int32, product.shape, 0) < rows
            hit = (row_ids == col_ids) & own & (index == diagonal)
            product = jnp.where(hit, product * jnp.float32(1.0 + damping), product)
        done[lax.rem(turn, 2)] = product
        start(stores(turn))
        for here in range(panel_count - 2):

            @pl.when(turn == here * tiles + tiles - 1)
            def fetch(later=loads[here + 2]):
                for copies in later:
                    start(copies)

        return carry

    lax.fori_loop(0, turns, turn_body, 0)
    for turn in range(max(0, turns - 2), turns):
        wait(stores(turn))
    wait(puts)


def panels(out, left, rows, columns, pairs, ids, received=(), diagonal=None, part=None, width=None, sends=False):
    depth, width = pairs[0][0][0].shape[0], width or pairs[0][0][0].shape[1]
    sizes = tuple(tuple(len(half) for half in pair) for pair in pairs)
    args = [ids, left] + [array for pair in pairs for half in pair for array in half]
    args += [stack for stack, _ in received]
    aliases = {}
    if out is not None:
        aliases = {len(args): 0}
        args.append(out)
    anywhere = pl.BlockSpec(memory_space=pl.ANY)
    most = max(map(sum, sizes))
    tile = 512 if width % 512 == 0 else min(256, width)
    height = 2 * rows if sends else rows
    shapes = [jax.ShapeDtypeStruct((rows, columns), jnp.float32)]
    if sends:
        shapes.append(jax.ShapeDtypeStruct((len(pairs), rows, width), jnp.float32))
    stacked = max([stack.shape[0] for stack, _ in received], default=1)
    outs = pl.pallas_call(
        functools.partial(
            panel_kernel,
            sizes,
            diagonal,
            part or (0, width),
            tuple(place for _, place in received),
            width,
            tile,
            sends,
        ),
        out_shape=shapes,
        in_specs=[pl.BlockSpec(memory_space=pltpu.SMEM)] + [anywhere] * (len(args) - 1),
        out_specs=[anywhere] * len(shapes),
        scratch_shapes=[
            pltpu.VMEM((height, left.shape[1]), left.dtype),
            pltpu.VMEM((2, most, depth, width), jnp.float32),
            pltpu.VMEM((2, height, tile), jnp.float32),
            pltpu.SemaphoreType.DMA,
            pltpu.SemaphoreType.DMA((2, most, width // tile)),
            pltpu.SemaphoreType.DMA((2, 2)),
            pltpu.SemaphoreType.DMA((max(1, len(received)), stacked, 2)),
            *[pltpu.VMEM(stack.shape, jnp.float32) for stack, _ in received],
        ],
        input_output_aliases=aliases,
        compiler_params=pltpu.CompilerParams(vmem_limit_bytes=VMEM_BYTES),
        cost_estimate=pl.CostEstimate(
            flops=30 * height * left.shape[1] * width * len(pairs),
            bytes_accessed=4 * width * len(pairs) * (height + 2 * depth),
            transcendentals=0,
        ),
        name="panels",
    )(*args)
    return outs if sends else outs[0]


def choose_kernel(jobs, flag_ref, *refs):
    outs = refs[-1 - 2 * len(jobs) : -1 - len(jobs)]
    stages, sems = refs[-1 - len(jobs) : -1], refs[-1]
    pieces = sems.shape[1]
    rows = [pl.ds(k * (stages[0].shape[0] // pieces), stages[0].shape[0] // pieces) for k in range(pieces)]

    def fetch(job, k, pick):
        first, columns = jobs[job], pl.ds(jobs[job][2], stages[job].shape[1])
        return pltpu.make_async_copy(refs[first[pick]].at[rows[k], columns], stages[job].at[rows[k]], sems.at[job, k, 0])

    def put(job, k):
        return pltpu.make_async_copy(stages[job].at[rows[k]], outs[job].at[rows[k]], sems.at[job, k, 1])

    every = [(job, k) for job in range(len(jobs)) for k in range(pieces)]
    for pick in range(2):

        @pl.when(flag_ref[0] == 1 - pick)
        def start(pick=pick):
            for job, k in every:
                fetch(job, k, pick).start()

    for job, k in every:
        fetch(job, k, 0).wait()
        put(job, k).start()
    for job, k in every:
        put(job, k).wait()


def choose(flag, operands, jobs):
    rows = operands[0].shape[0]
    anywhere = pl.BlockSpec(memory_space=pltpu.HBM)
    shapes = [(rows, job[3]) for job in jobs]
    return pl.pallas_call(
        functools.partial(choose_kernel, [job[:3] for job in jobs]),
        out_shape=[jax.ShapeDtypeStruct(shape, jnp.float32) for shape in shapes],
        in_specs=[pl.BlockSpec(memory_space=pltpu.SMEM)] + [anywhere] * len(operands),
        out_specs=[anywhere] * len(jobs),
        scratch_shapes=[pltpu.VMEM(shape, jnp.float32) for shape in shapes] + [pltpu.SemaphoreType.DMA((len(jobs), 3, 2))],
        compiler_params=pltpu.CompilerParams(vmem_limit_bytes=VMEM_BYTES),
        cost_estimate=pl.CostEstimate(flops=0, bytes_accessed=4 * operands[0].size, transcendentals=0),
        name="choose",
    )(flag, *operands)


def place_kernel(placed, ids_ref, *refs):
    received, out_ref, place_sem, stages = refs[: len(placed)], refs[len(placed) + 1], refs[len(placed) + 2], refs[len(placed) + 3 :]
    fetches, puts, at = [], [], 0
    for number, (from_ref, stage, (begin, size)) in enumerate(zip(received, stages, placed)):
        for index in range(from_ref.shape[0]):
            column = pl.multiple_of(ids_ref[at] * size + begin, 128)
            target = out_ref.at[:, pl.ds(column, from_ref.shape[-1])]
            fetches.append(pltpu.make_async_copy(from_ref.at[index], stage.at[index], place_sem.at[number, index, 0]))
            puts.append(pltpu.make_async_copy(stage.at[index], target, place_sem.at[number, index, 1]))
            at += 1
    for fetch in fetches:
        fetch.start()
    for fetch, put in zip(fetches, puts):
        fetch.wait()
        put.start()
    for put in puts:
        put.wait()


def place(out, received, ids):
    stacks = [stack for stack, _ in received]
    anywhere = pl.BlockSpec(memory_space=pltpu.HBM)
    return pl.pallas_call(
        functools.partial(place_kernel, [part for _, part in received]),
        out_shape=jax.ShapeDtypeStruct(out.shape, out.dtype),
        in_specs=[pl.BlockSpec(memory_space=pltpu.SMEM)] + [anywhere] * (len(stacks) + 1),
        out_specs=anywhere,
        scratch_shapes=[pltpu.SemaphoreType.DMA((len(stacks), max(v.shape[0] for v in stacks), 2))]
        + [pltpu.VMEM(v.shape, v.dtype) for v in stacks],
        input_output_aliases={len(stacks) + 1: 0},
        compiler_params=pltpu.CompilerParams(vmem_limit_bytes=VMEM_BYTES),
        cost_estimate=pl.CostEstimate(flops=0, bytes_accessed=8 * sum(v.size for v in stacks), transcendentals=0),
        name="place",
    )(ids, *stacks, out)


def gathered(loop, grp, jacobian):
    rows_here = jacobian.shape[1] // grp
    me, side = lax.axis_index("loop"), lax.axis_index("grp")
    both = lax.all_gather(jacobian, "grp")
    everything = lax.all_gather(both, "loop")
    mine = lax.dynamic_slice_in_dim(both, side * rows_here, rows_here, axis=2)
    left = left_operand(mine[0], mine[1])
    out = None
    for turn in range(loop):
        panel = (me + turn) % loop
        pair = tuple((lax.dynamic_index_in_dim(everything, panel, keepdims=False)[g],) for g in range(2))
        ids = jnp.stack([panel, side * rows_here]).astype(jnp.int32)
        out = panels(out, left, rows_here, jacobian.shape[1] * loop, [pair], ids, diagonal=None if turn else 0)
    return out


def rounds(loop, grp, jacobian):
    width = jacobian.shape[1]
    rows_here, columns = width // grp, width * loop
    me, side = lax.axis_index("loop"), lax.axis_index("grp")
    z, y, core = me // 4, (me // 2) % 2, me % 2

    along_x = lambda v: lax.ppermute(v, "grp", [(0, 1), (1, 0)])
    along_y = lambda v: lax.ppermute(v, "loop", [(i, i ^ 2) for i in range(16)])
    pair_z = lambda v: lax.ppermute(v, "loop", [(i, i ^ 4) for i in range(16)])
    mid_z = lambda v: lax.ppermute(
        v, "loop", [(i, i + 4) for i in range(4, 8)] + [(i + 4, i) for i in range(4, 8)]
    )
    swap = lambda v: lax.ppermute(v, "loop", [(i, i ^ 1) for i in range(16)])
    together = lax.optimization_barrier
    after = lambda value, *first: together((value, first))[0]

    mate_z = z ^ 1
    near_z = jnp.where(z < 2, 2, 1)
    far_z = jnp.where(z < 2, 3, 0)
    shift = side * rows_here
    places = [(z, y), (z, 1 - y), (near_z, y), (mate_z, 1 - y), (mate_z, y), (near_z, 1 - y), (far_z, y), (far_z, 1 - y)]
    own = [zz * 4 + yy * 2 + core for zz, yy in places]
    other = [zz * 4 + yy * 2 + 1 - core for zz, yy in places]
    number = lambda *numbers: jnp.stack(numbers).astype(jnp.int32)
    ids = tuple(
        number(*n)
        for n in (
            own[:2] + [shift],
            own[2:4],
            own[4:6],
            own[6:] + other[2:4],
            own[6:] + other[4:6],
        )
    )
    put = number(*other[:2]), number(*other[6:], *other[6:])
    outer = number((z == 0) | (z == 3))
    step = lambda out, left, turn, pairs, **kw: panels(out, left, rows_here, columns, pairs, ids[turn], **kw)
    whole, cut = (0, width), width * 3 // 4

    c = jacobian
    x_self, mid0, c_mate, y_self = along_x(c), mid_z(c), pair_z(c), along_y(c)
    own_columns = lambda v: lax.dynamic_slice_in_dim(v, shift, rows_here, axis=1)
    own_c = own_columns(c)
    own_c_o = swap(own_c)
    mid0, own_c, own_c_o, ids, put, outer = together((mid0, own_c, own_c_o, ids, put, outer))

    pair1 = pair_z(after(mid0, c_mate))
    mid1 = mid_z(c_mate)
    y_mate = along_y(after(c_mate, y_self))
    d_self = along_x(after(y_self, x_self))
    own_x = own_columns(x_self)
    left = left_operand(own_c, own_x, own_c_o, swap(own_x))

    (c_near,) = choose(outer, (after(pair1, left), mid0), [(0, 1, 0, width)])
    d_mate = pair_z(after(d_self, pair1, left))
    y_near = along_y(after(c_near, y_mate))
    x_near = along_x(after(c_near, d_self))
    out, send2 = step(None, left, 0, [((c,), (x_self,)), ((y_self,), (d_self,))], diagonal=0, sends=True)

    mid3 = mid_z(after(d_mate, out))
    pair3 = pair_z(after(mid1, d_mate, out))
    d_near = along_y(after(x_near, y_near))
    x_mate = along_x(after(c_mate, x_near))
    out, send3 = step(out, left, 1, [((c_near,), (x_near,)), ((y_mate,), (d_mate,))], sends=True)
    out = place(out, ((swap(send2), whole),), put[0])

    rest = width - cut
    early_c, early_3 = choose(outer, (after(pair3, out), mid1, mid3), [(0, 1, 0, cut), (2, 2, 0, cut)])
    x_early = along_x(after(early_c, x_mate))
    d_early = pair_z(early_3)
    y_early = along_y(after(early_c, d_near))
    out, send4 = step(out, left, 2, [((c_mate,), (x_mate,)), ((y_near,), (d_near,))], sends=True)
    late_c, late_3 = choose(outer, (after(pair3, out), mid1, mid3), [(0, 1, cut, rest), (2, 2, cut, rest)])
    x_early, y_early, d_early, late_c, late_3, out = together((x_early, y_early, d_early, late_c, late_3, out))

    x_late = along_x(after(late_c, x_early))
    d_late = pair_z(after(late_3, d_early))
    y_late = along_y(after(late_c, y_early))
    pairs = [((early_c,), (x_early,)), ((y_early,), (d_early, early_3))]
    out, send5 = step(out, left, 3, pairs, received=((swap(send3), whole),), part=whole, sends=True)
    x_late, y_late, d_late, out = together((x_late, y_late, d_late, out))

    pairs = [((late_c,), (x_late,)), ((y_late,), (d_late, late_3))]
    out, send6 = step(out, left, 4, pairs, received=((swap(send4), whole),), part=(cut, width), sends=True)
    return place(out, ((swap(send5), whole), (swap(send6), (cut, width))), put[1])


def solution(mesh):
    loop, grp = mesh.shape["loop"], mesh.shape["grp"]
    plan = rounds if (loop, grp) == (16, 2) else gathered
    return jax.shard_map(
        functools.partial(plan, loop, grp),
        mesh=mesh,
        in_specs=(P("grp", "loop"),),
        out_specs=P(("loop", "grp"), None),
        check_vma=False,
    )
```

```python
import functools

import jax
import jax.numpy as jnp
from jax import lax
from jax.experimental import pallas as pl
from jax.experimental.pallas import tpu as pltpu
from jax.sharding import PartitionSpec as P

damping = 0.1
VMEM_BYTES = 63 * 1024 * 1024 + 512 * 1024
COST = 1024


def split_high_low(value):
    high = value.astype(jnp.bfloat16)
    low = (value - high.astype(jnp.float32)).astype(jnp.bfloat16)
    return high, low


def left_kernel(*refs):
    left_ref = refs[-1]
    depth, rows = refs[0].shape
    for block in range(len(refs) // 2):
        for place, ref in enumerate(refs[2 * block : 2 * block + 2]):
            high, low = split_high_low(ref[...].T)
            for part, piece in enumerate((high, low)):
                target = pl.ds(rows * block, rows), pl.ds(2 * depth * part + depth * place, depth)
                left_ref[target] = piece


def left_operand(*halves):
    depth, rows = halves[0].shape
    shape = rows * (len(halves) // 2), 4 * depth
    return pl.pallas_call(
        left_kernel,
        out_shape=jax.ShapeDtypeStruct(shape, jnp.bfloat16),
        compiler_params=pltpu.CompilerParams(vmem_limit_bytes=VMEM_BYTES),
        cost_estimate=pl.CostEstimate(flops=COST, bytes_accessed=COST, transcendentals=0),
        name="left_operand",
    )(*halves)


def panel_kernel(sizes, diagonal, part, placed, width, tile, sends, ids_ref, left_hbm, *refs):
    count = sum(map(sum, sizes))
    blocks, received = refs[:count], refs[count : count + len(placed)]
    left_ref, held, done, left_sem, load_sem, store_sem, place_sem = refs[-7 - len(placed) : len(refs) - len(placed)]
    stages = refs[len(refs) - len(placed) :]
    out_ref, send_ref = refs[-9 - len(placed) : -7 - len(placed)] if sends else (refs[-8 - len(placed)], None)
    rows, (first, whole) = out_ref.shape[0], part
    tiles, panel_count = width // tile, len(sizes)
    turns = panel_count * tiles
    most = max(map(sum, sizes))
    height, depth = done.shape[1], left_ref.shape[1] // 2
    left = [left_ref.at[:, pl.ds(k * depth, depth)] for k in range(2)]
    left_copy = pltpu.make_async_copy(left_hbm.at[pl.ds(0, height)], left_ref, left_sem)

    loads, at = [], 0
    for index, counts in enumerate(sizes):
        loads.append([[] for _ in range(tiles)])
        for place in range(sum(counts)):
            skip = first if blocks[at].shape[1] > width else 0
            for t in range(tiles):
                source = blocks[at].at[:, pl.ds(skip + t * tile, tile)]
                target = held.at[index % 2, place, :, pl.ds(t * tile, tile)]
                loads[index][t].append(pltpu.make_async_copy(source, target, load_sem.at[index % 2, place, t]))
            at += 1
    fetches, puts, at = [], [], panel_count
    for number, (from_ref, stage, (begin, size)) in enumerate(zip(received, stages, placed)):
        for index in range(from_ref.shape[0]):
            column = pl.multiple_of(ids_ref[at] * size + begin, 128)
            target = out_ref.at[:, pl.ds(column, from_ref.shape[-1])]
            fetches.append(pltpu.make_async_copy(from_ref.at[index], stage.at[index], place_sem.at[number, index, 0]))
            puts.append(pltpu.make_async_copy(stage.at[index], target, place_sem.at[number, index, 1]))
            at += 1

    def stores(turn):
        index, column = turn // tiles, pl.multiple_of(lax.rem(turn, tiles) * tile, 128)
        slot = lax.rem(turn, 2)
        place = pl.multiple_of(ids_ref[index] * whole + first + column, 128)
        copies = [(done.at[slot, pl.ds(0, rows)], out_ref.at[:, pl.ds(place, tile)], store_sem.at[slot, 0])]
        if sends:
            target = send_ref.at[index, :, pl.ds(column, tile)]
            copies.append((done.at[slot, pl.ds(rows, rows)], target, store_sem.at[slot, 1]))
        return [pltpu.make_async_copy(*copy) for copy in copies]

    def start(copies):
        for copy in copies:
            copy.start()

    def wait(copies):
        for copy in copies:
            copy.wait()

    start(loads[0][0] + [left_copy])
    for copies in loads[0][1:]:
        start(copies)
    left_copy.wait()

    def turn_body(turn, carry):
        index, column = turn // tiles, pl.multiple_of(lax.rem(turn, tiles) * tile, 128)
        slot = lax.rem(index, 2)
        for here in range(turns):

            @pl.when(turn == here)
            def arrive(here=here):
                wait(loads[here // tiles][here % tiles])
                if here == 0:
                    for copies in loads[1] if panel_count > 1 else []:
                        start(copies)
                    start(fetches)

        @pl.when(turn >= 2)
        def free():
            wait(stores(turn - 2))

        @pl.when(turn == turns // 2)
        def put():
            wait(fetches)
            start(puts)

        block = [held[slot, k, :, pl.ds(column, tile)] for k in range(most)]
        if most > 2:
            extra = functools.reduce(jnp.logical_or, [index == i for i, n in enumerate(sizes) if sum(n) > 2])
            block[1] = jnp.where(extra & (ids_ref[ids_ref.shape[0] - 1] == 0), block[2], block[1])
        halves = [split_high_low(value) for value in block[:2]]
        high, low = (jnp.concatenate(pieces, axis=0) for pieces in zip(*halves))
        dot = functools.partial(jnp.dot, preferred_element_type=jnp.float32)
        product = dot(left[0][...], high) + dot(left[0][...], low) + dot(left[1][...], high)
        if diagonal is not None:
            row_ids = lax.broadcasted_iota(jnp.int32, product.shape, 0) + ids_ref[ids_ref.shape[0] - 1]
            col_ids = lax.broadcasted_iota(jnp.int32, product.shape, 1) + column
            own = lax.broadcasted_iota(jnp.int32, product.shape, 0) < rows
            hit = (row_ids == col_ids) & own & (index == diagonal)
            product = jnp.where(hit, product * jnp.float32(1.0 + damping), product)
        done[lax.rem(turn, 2)] = product
        start(stores(turn))
        for here in range(panel_count - 2):

            @pl.when(turn == here * tiles + tiles - 1)
            def fetch(later=loads[here + 2]):
                for copies in later:
                    start(copies)

        return carry

    lax.fori_loop(0, turns, turn_body, 0)
    for turn in range(max(0, turns - 2), turns):
        wait(stores(turn))
    wait(puts)


def panels(out, left, rows, columns, pairs, ids, received=(), diagonal=None, part=None, width=None, sends=False):
    depth, width = pairs[0][0][0].shape[0], width or pairs[0][0][0].shape[1]
    sizes = tuple(tuple(len(half) for half in pair) for pair in pairs)
    args = [ids, left] + [array for pair in pairs for half in pair for array in half]
    args += [stack for stack, _ in received]
    aliases = {}
    if out is not None:
        aliases = {len(args): 0}
        args.append(out)
    anywhere = pl.BlockSpec(memory_space=pl.ANY)
    most = max(map(sum, sizes))
    tile = 512 if width % 512 == 0 else 256 if width % 256 == 0 else width
    height = 2 * rows if sends else rows
    shapes = [jax.ShapeDtypeStruct((rows, columns), jnp.float32)]
    if sends:
        shapes.append(jax.ShapeDtypeStruct((len(pairs), rows, width), jnp.float32))
    stacked = max([stack.shape[0] for stack, _ in received], default=1)
    outs = pl.pallas_call(
        functools.partial(
            panel_kernel,
            sizes,
            diagonal,
            part or (0, width),
            tuple(place for _, place in received),
            width,
            tile,
            sends,
        ),
        out_shape=shapes,
        in_specs=[pl.BlockSpec(memory_space=pltpu.SMEM)] + [anywhere] * (len(args) - 1),
        out_specs=[anywhere] * len(shapes),
        scratch_shapes=[
            pltpu.VMEM((height, left.shape[1]), left.dtype),
            pltpu.VMEM((2, most, depth, width), jnp.float32),
            pltpu.VMEM((2, height, tile), jnp.float32),
            pltpu.SemaphoreType.DMA,
            pltpu.SemaphoreType.DMA((2, most, width // tile)),
            pltpu.SemaphoreType.DMA((2, 2)),
            pltpu.SemaphoreType.DMA((max(1, len(received)), stacked, 2)),
            *[pltpu.VMEM(stack.shape, jnp.float32) for stack, _ in received],
        ],
        input_output_aliases=aliases,
        compiler_params=pltpu.CompilerParams(vmem_limit_bytes=VMEM_BYTES),
        cost_estimate=pl.CostEstimate(
            flops=30 * height * left.shape[1] * width * len(pairs),
            bytes_accessed=4 * width * len(pairs) * (height + 2 * depth),
            transcendentals=0,
        ),
        name="panels",
    )(*args)
    return outs if sends else outs[0]


def choose_kernel(jobs, flag_ref, *refs):
    outs = refs[-1 - 2 * len(jobs) : -1 - len(jobs)]
    stages, sems = refs[-1 - len(jobs) : -1], refs[-1]
    pieces = sems.shape[1]
    rows = [pl.ds(k * (stages[0].shape[0] // pieces), stages[0].shape[0] // pieces) for k in range(pieces)]

    def fetch(job, k, pick):
        first, columns = jobs[job], pl.ds(jobs[job][2], stages[job].shape[1])
        return pltpu.make_async_copy(refs[first[pick]].at[rows[k], columns], stages[job].at[rows[k]], sems.at[job, k, 0])

    def put(job, k):
        return pltpu.make_async_copy(stages[job].at[rows[k]], outs[job].at[rows[k]], sems.at[job, k, 1])

    every = [(job, k) for job in range(len(jobs)) for k in range(pieces)]
    for pick in range(2):

        @pl.when(flag_ref[0] == 1 - pick)
        def start(pick=pick):
            for job, k in every:
                fetch(job, k, pick).start()

    for job, k in every:
        fetch(job, k, 0).wait()
        put(job, k).start()
    for job, k in every:
        put(job, k).wait()


def choose(flag, operands, jobs):
    rows = operands[0].shape[0]
    anywhere = pl.BlockSpec(memory_space=pltpu.HBM)
    shapes = [(rows, job[3]) for job in jobs]
    return pl.pallas_call(
        functools.partial(choose_kernel, [job[:3] for job in jobs]),
        out_shape=[jax.ShapeDtypeStruct(shape, jnp.float32) for shape in shapes],
        in_specs=[pl.BlockSpec(memory_space=pltpu.SMEM)] + [anywhere] * len(operands),
        out_specs=[anywhere] * len(jobs),
        scratch_shapes=[pltpu.VMEM(shape, jnp.float32) for shape in shapes] + [pltpu.SemaphoreType.DMA((len(jobs), 3, 2))],
        compiler_params=pltpu.CompilerParams(vmem_limit_bytes=VMEM_BYTES),
        cost_estimate=pl.CostEstimate(flops=0, bytes_accessed=4 * operands[0].size, transcendentals=0),
        name="choose",
    )(flag, *operands)


def place_kernel(placed, ids_ref, *refs):
    received, out_ref, place_sem, stages = refs[: len(placed)], refs[len(placed) + 1], refs[len(placed) + 2], refs[len(placed) + 3 :]
    fetches, puts, at = [], [], 0
    for number, (from_ref, stage, (begin, size)) in enumerate(zip(received, stages, placed)):
        for index in range(from_ref.shape[0]):
            column = pl.multiple_of(ids_ref[at] * size + begin, 128)
            target = out_ref.at[:, pl.ds(column, from_ref.shape[-1])]
            fetches.append(pltpu.make_async_copy(from_ref.at[index], stage.at[index], place_sem.at[number, index, 0]))
            puts.append(pltpu.make_async_copy(stage.at[index], target, place_sem.at[number, index, 1]))
            at += 1
    for fetch in fetches:
        fetch.start()
    for fetch, put in zip(fetches, puts):
        fetch.wait()
        put.start()
    for put in puts:
        put.wait()


def place(out, received, ids):
    stacks = [stack for stack, _ in received]
    anywhere = pl.BlockSpec(memory_space=pltpu.HBM)
    return pl.pallas_call(
        functools.partial(place_kernel, [part for _, part in received]),
        out_shape=jax.ShapeDtypeStruct(out.shape, out.dtype),
        in_specs=[pl.BlockSpec(memory_space=pltpu.SMEM)] + [anywhere] * (len(stacks) + 1),
        out_specs=anywhere,
        scratch_shapes=[pltpu.SemaphoreType.DMA((len(stacks), max(v.shape[0] for v in stacks), 2))]
        + [pltpu.VMEM(v.shape, v.dtype) for v in stacks],
        input_output_aliases={len(stacks) + 1: 0},
        compiler_params=pltpu.CompilerParams(vmem_limit_bytes=VMEM_BYTES),
        cost_estimate=pl.CostEstimate(flops=0, bytes_accessed=8 * sum(v.size for v in stacks), transcendentals=0),
        name="place",
    )(ids, *stacks, out)


def gathered(loop, grp, jacobian):
    rows_here = jacobian.shape[1] // grp
    me, side = lax.axis_index("loop"), lax.axis_index("grp")
    both = lax.all_gather(jacobian, "grp")
    everything = lax.all_gather(both, "loop")
    mine = lax.dynamic_slice_in_dim(both, side * rows_here, rows_here, axis=2)
    left = left_operand(mine[0], mine[1])
    out = None
    for turn in range(loop):
        panel = (me + turn) % loop
        pair = tuple((lax.dynamic_index_in_dim(everything, panel, keepdims=False)[g],) for g in range(2))
        ids = jnp.stack([panel, side * rows_here]).astype(jnp.int32)
        out = panels(out, left, rows_here, jacobian.shape[1] * loop, [pair], ids, diagonal=None if turn else 0)
    return out


def rounds(loop, grp, jacobian):
    width = jacobian.shape[1]
    rows_here, columns = width // grp, width * loop
    me, side = lax.axis_index("loop"), lax.axis_index("grp")
    z, y, core = me // 4, (me // 2) % 2, me % 2

    along_x = lambda v: lax.ppermute(v, "grp", [(0, 1), (1, 0)])
    along_y = lambda v: lax.ppermute(v, "loop", [(i, i ^ 2) for i in range(16)])
    pair_z = lambda v: lax.ppermute(v, "loop", [(i, i ^ 4) for i in range(16)])
    inner = [(i, i + 4) for i in range(4, 8)] + [(i + 4, i) for i in range(4, 8)]
    mid_z = lambda v: lax.ppermute(v, "loop", inner)
    mid_z_all = lambda v: lax.ppermute(v, "loop", inner + [(i, i ^ 1) for i in (0, 1, 2, 3, 12, 13, 14, 15)])
    swap = lambda v: lax.ppermute(v, "loop", [(i, i ^ 1) for i in range(16)])
    together = lax.optimization_barrier
    after = lambda value, *first: together((value, first))[0]

    mate_z = z ^ 1
    near_z = jnp.where(z < 2, 2, 1)
    far_z = jnp.where(z < 2, 3, 0)
    shift = side * rows_here
    places = [(z, y), (z, 1 - y), (near_z, y), (mate_z, 1 - y), (mate_z, y), (near_z, 1 - y), (far_z, y), (far_z, 1 - y)]
    own = [zz * 4 + yy * 2 + core for zz, yy in places]
    other = [zz * 4 + yy * 2 + 1 - core for zz, yy in places]
    number = lambda *numbers: jnp.stack([jnp.int32(n) for n in numbers])
    outer = jnp.int32((z == 0) | (z == 3))
    ids = tuple(
        number(*n)
        for n in (
            own[:2] + [shift],
            own[2:4],
            own[4:6],
            own[6:] + other[2:4] + [outer],
            own[6:] + other[4:6] + [outer],
        )
    )
    put = number(*other[:2]), number(*other[6:])
    outer = number(outer)
    step = lambda out, left, turn, pairs, **kw: panels(out, left, rows_here, columns, pairs, ids[turn], **kw)
    whole, cut = (0, width), width * 5 // 8

    c = jacobian
    x_self, mid0, c_mate, y_self = along_x(c), mid_z(c), pair_z(c), along_y(c)
    own_columns = lambda v: lax.dynamic_slice_in_dim(v, shift, rows_here, axis=1)
    own_c = own_columns(c)
    own_c_o = swap(own_c)
    mid0, own_c, own_c_o, ids, put, outer = together((mid0, own_c, own_c_o, ids, put, outer))

    pair1 = pair_z(after(mid0, c_mate))
    mid1 = mid_z(c_mate)
    y_mate = along_y(after(c_mate, y_self))
    d_self = along_x(after(y_self, x_self))
    own_x = own_columns(x_self)
    left = left_operand(own_c, own_x, own_c_o, swap(own_x))

    (c_near,) = choose(outer, (after(pair1, left), mid0), [(0, 1, 0, width)])
    d_mate = pair_z(after(d_self, pair1, left))
    y_near = along_y(after(c_near, y_mate))
    x_near = along_x(after(c_near, d_self))
    out, send2 = step(None, left, 0, [((c,), (x_self,)), ((y_self,), (d_self,))], diagonal=0, sends=True)

    mid3 = mid_z_all(after(d_mate, out))
    pair3 = pair_z(after(mid1, d_mate, out))
    d_near = along_y(after(x_near, y_near))
    x_mate = along_x(after(c_mate, x_near))
    out, send3 = step(out, left, 1, [((c_near,), (x_near,)), ((y_mate,), (d_mate,))], sends=True)
    out = place(out, ((swap(send2), whole),), put[0])

    rest = width - cut
    early_c, early_3, late_c, late_3 = choose(
        outer,
        (after(pair3, out), mid1, mid3),
        [(0, 1, 0, cut), (2, 2, 0, cut), (0, 1, cut, rest), (2, 2, cut, rest)],
    )
    x_early = along_x(after(early_c, x_mate))
    d_early = pair_z(early_3)
    y_early = along_y(after(early_c, d_near))
    out, send4 = step(out, left, 2, [((c_mate,), (x_mate,)), ((y_near,), (d_near,))], sends=True)
    x_early, y_early, d_early, out = together((x_early, y_early, d_early, out))

    x_late = along_x(after(late_c, x_early))
    d_late = pair_z(after(late_3, d_early))
    y_late = along_y(after(late_c, y_early))
    pairs = [((early_c,), (x_early,)), ((y_early,), (d_early, early_3))]
    out, send5 = step(out, left, 3, pairs, received=((swap(send3), whole),), part=whole, sends=True)
    x_late, y_late, d_late, out = together((x_late, y_late, d_late, out))

    pairs = [((late_c,), (x_late,)), ((y_late,), (d_late, late_3))]
    out, send6 = step(out, left, 4, pairs, received=((swap(send4), whole),), part=(cut, width), sends=True)
    out = place(out, ((swap(send5), whole),), put[1])
    return place(out, ((swap(send6), (cut, width)),), put[1])


def solution(mesh):
    loop, grp = mesh.shape["loop"], mesh.shape["grp"]
    plan = rounds if (loop, grp) == (16, 2) else gathered
    return jax.shard_map(
        functools.partial(plan, loop, grp),
        mesh=mesh,
        in_specs=(P("grp", "loop"),),
        out_specs=P(("loop", "grp"), None),
        check_vma=False,
    )
```

```python
import functools

import jax
import jax.numpy as jnp
from jax import lax
from jax.experimental import pallas as pl
from jax.experimental.pallas import tpu as pltpu
from jax.sharding import PartitionSpec as P

damping = 0.1
VMEM_BYTES = 63 * 1024 * 1024 + 512 * 1024
COST = 1024


def split_high_low(value):
    high = value.astype(jnp.bfloat16)
    low = (value - high.astype(jnp.float32)).astype(jnp.bfloat16)
    return high, low


def left_kernel(*refs):
    left_ref = refs[-1]
    depth, rows = refs[0].shape
    for block in range(len(refs) // 2):
        for place, ref in enumerate(refs[2 * block : 2 * block + 2]):
            high, low = split_high_low(ref[...].T)
            for part, piece in enumerate((high, low)):
                target = pl.ds(rows * block, rows), pl.ds(2 * depth * part + depth * place, depth)
                left_ref[target] = piece


def left_operand(*halves):
    depth, rows = halves[0].shape
    shape = rows * (len(halves) // 2), 4 * depth
    return pl.pallas_call(
        left_kernel,
        out_shape=jax.ShapeDtypeStruct(shape, jnp.bfloat16),
        compiler_params=pltpu.CompilerParams(vmem_limit_bytes=VMEM_BYTES),
        cost_estimate=pl.CostEstimate(flops=COST, bytes_accessed=COST, transcendentals=0),
        name="left_operand",
    )(*halves)


def panel_kernel(sizes, diagonal, part, placed, width, tile, sends, ids_ref, left_hbm, *refs):
    count = sum(map(sum, sizes))
    blocks, received = refs[:count], refs[count : count + len(placed)]
    left_ref, held, done, left_sem, load_sem, store_sem, place_sem = refs[-7 - len(placed) : len(refs) - len(placed)]
    stages = refs[len(refs) - len(placed) :]
    out_ref, send_ref = refs[-9 - len(placed) : -7 - len(placed)] if sends else (refs[-8 - len(placed)], None)
    rows, (first, whole) = out_ref.shape[0], part
    tiles, panel_count = width // tile, len(sizes)
    turns = panel_count * tiles
    most = max(map(sum, sizes))
    height, depth = done.shape[1], left_ref.shape[1] // 2
    left = [left_ref.at[:, pl.ds(k * depth, depth)] for k in range(2)]
    left_copies = [
        pltpu.make_async_copy(left_hbm.at[pl.ds(0, height), pl.ds(k * depth, depth)], left[k], left_sem.at[k])
        for k in range(2)
    ]

    loads, at = [], 0
    for index, counts in enumerate(sizes):
        loads.append([[] for _ in range(tiles)])
        for place in range(sum(counts)):
            skip = first if blocks[at].shape[1] > width else 0
            for t in range(tiles):
                source = blocks[at].at[:, pl.ds(skip + t * tile, tile)]
                target = held.at[index % 2, place, :, pl.ds(t * tile, tile)]
                loads[index][t].append(pltpu.make_async_copy(source, target, load_sem.at[index % 2, place, t]))
            at += 1
    fetches, puts, at = [], [], panel_count
    for number, (from_ref, stage, (begin, size)) in enumerate(zip(received, stages, placed)):
        for index in range(from_ref.shape[0]):
            column = pl.multiple_of(ids_ref[at] * size + begin, 128)
            target = out_ref.at[:, pl.ds(column, from_ref.shape[-1])]
            fetches.append(pltpu.make_async_copy(from_ref.at[index], stage.at[index], place_sem.at[number, index, 0]))
            puts.append(pltpu.make_async_copy(stage.at[index], target, place_sem.at[number, index, 1]))
            at += 1

    def stores(turn):
        index, column = turn // tiles, pl.multiple_of(lax.rem(turn, tiles) * tile, 128)
        slot = lax.rem(turn, 2)
        place = pl.multiple_of(ids_ref[index] * whole + first + column, 128)
        copies = [(done.at[slot, pl.ds(0, rows)], out_ref.at[:, pl.ds(place, tile)], store_sem.at[slot, 0])]
        if sends:
            target = send_ref.at[index, :, pl.ds(column, tile)]
            copies.append((done.at[slot, pl.ds(rows, rows)], target, store_sem.at[slot, 1]))
        return [pltpu.make_async_copy(*copy) for copy in copies]

    def start(copies):
        for copy in copies:
            copy.start()

    def wait(copies):
        for copy in copies:
            copy.wait()

    start(loads[0][0] + left_copies)
    for copies in loads[0][1:]:
        start(copies)
    left_copies[0].wait()
    if tile != 512:
        left_copies[1].wait()

    def turn_body(turn, carry):
        index, column = turn // tiles, pl.multiple_of(lax.rem(turn, tiles) * tile, 128)
        slot = lax.rem(index, 2)
        for here in range(turns):

            @pl.when(turn == here)
            def arrive(here=here):
                wait(loads[here // tiles][here % tiles])
                if here == 0:
                    for copies in loads[1] if panel_count > 1 else []:
                        start(copies)
                    start(fetches)

        @pl.when(turn >= 2)
        def free():
            wait(stores(turn - 2))

        @pl.when(turn == turns // 2)
        def put():
            wait(fetches)
            start(puts)

        block = [held[slot, k, :, pl.ds(column, tile)] for k in range(most)]
        if most > 2:
            extra = functools.reduce(jnp.logical_or, [index == i for i, n in enumerate(sizes) if sum(n) > 2])
            block[1] = jnp.where(extra & (ids_ref[ids_ref.shape[0] - 1] == 0), block[2], block[1])
        halves = [split_high_low(value) for value in block[:2]]
        high, low = (jnp.concatenate(pieces, axis=0) for pieces in zip(*halves))
        dot = functools.partial(jnp.dot, preferred_element_type=jnp.float32)
        product = dot(left[0][...], high) + dot(left[0][...], low)
        if tile == 512:

            @pl.when(turn == 0)
            def rest_of_left():
                left_copies[1].wait()

        product += dot(left[1][...], high)
        if diagonal is not None:
            row_ids = lax.broadcasted_iota(jnp.int32, product.shape, 0) + ids_ref[ids_ref.shape[0] - 1]
            col_ids = lax.broadcasted_iota(jnp.int32, product.shape, 1) + column
            own = lax.broadcasted_iota(jnp.int32, product.shape, 0) < rows
            hit = (row_ids == col_ids) & own & (index == diagonal)
            product = jnp.where(hit, product * jnp.float32(1.0 + damping), product)
        done[lax.rem(turn, 2)] = product
        start(stores(turn))
        for here in range(panel_count - 2):

            @pl.when(turn == here * tiles + tiles - 1)
            def fetch(later=loads[here + 2]):
                for copies in later:
                    start(copies)

        return carry

    lax.fori_loop(0, turns, turn_body, 0)
    for turn in range(max(0, turns - 2), turns):
        wait(stores(turn))
    wait(puts)


def panels(out, left, rows, columns, pairs, ids, received=(), diagonal=None, part=None, width=None, sends=False):
    depth, width = pairs[0][0][0].shape[0], width or pairs[0][0][0].shape[1]
    sizes = tuple(tuple(len(half) for half in pair) for pair in pairs)
    args = [ids, left] + [array for pair in pairs for half in pair for array in half]
    args += [stack for stack, _ in received]
    aliases = {}
    if out is not None:
        aliases = {len(args): 0}
        args.append(out)
    anywhere = pl.BlockSpec(memory_space=pl.ANY)
    most = max(map(sum, sizes))
    tile = 512 if width % 512 == 0 else 256 if width % 256 == 0 else width
    height = 2 * rows if sends else rows
    shapes = [jax.ShapeDtypeStruct((rows, columns), jnp.float32)]
    if sends:
        shapes.append(jax.ShapeDtypeStruct((len(pairs), rows, width), jnp.float32))
    stacked = max([stack.shape[0] for stack, _ in received], default=1)
    outs = pl.pallas_call(
        functools.partial(
            panel_kernel,
            sizes,
            diagonal,
            part or (0, width),
            tuple(place for _, place in received),
            width,
            tile,
            sends,
        ),
        out_shape=shapes,
        in_specs=[pl.BlockSpec(memory_space=pltpu.SMEM)] + [anywhere] * (len(args) - 1),
        out_specs=[anywhere] * len(shapes),
        scratch_shapes=[
            pltpu.VMEM((height, left.shape[1]), left.dtype),
            pltpu.VMEM((2, most, depth, width), jnp.float32),
            pltpu.VMEM((2, height, tile), jnp.float32),
            pltpu.SemaphoreType.DMA((2,)),
            pltpu.SemaphoreType.DMA((2, most, width // tile)),
            pltpu.SemaphoreType.DMA((2, 2)),
            pltpu.SemaphoreType.DMA((max(1, len(received)), stacked, 2)),
            *[pltpu.VMEM(stack.shape, jnp.float32) for stack, _ in received],
        ],
        input_output_aliases=aliases,
        compiler_params=pltpu.CompilerParams(vmem_limit_bytes=VMEM_BYTES),
        cost_estimate=pl.CostEstimate(
            flops=30 * height * left.shape[1] * width * len(pairs),
            bytes_accessed=4 * width * len(pairs) * (height + 2 * depth),
            transcendentals=0,
        ),
        name="panels",
    )(*args)
    return outs if sends else outs[0]


def choose_kernel(jobs, flag_ref, *refs):
    outs = refs[-1 - 2 * len(jobs) : -1 - len(jobs)]
    stages, sems = refs[-1 - len(jobs) : -1], refs[-1]
    pieces = sems.shape[1]
    rows = [pl.ds(k * (stages[0].shape[0] // pieces), stages[0].shape[0] // pieces) for k in range(pieces)]

    def fetch(job, k, pick):
        first, columns = jobs[job], pl.ds(jobs[job][2], stages[job].shape[1])
        return pltpu.make_async_copy(refs[first[pick]].at[rows[k], columns], stages[job].at[rows[k]], sems.at[job, k, 0])

    def put(job, k):
        return pltpu.make_async_copy(stages[job].at[rows[k]], outs[job].at[rows[k]], sems.at[job, k, 1])

    every = [(job, k) for job in range(len(jobs)) for k in range(pieces)]
    for pick in range(2):

        @pl.when(flag_ref[0] == 1 - pick)
        def start(pick=pick):
            for job, k in every:
                fetch(job, k, pick).start()

    for job, k in every:
        fetch(job, k, 0).wait()
        put(job, k).start()
    for job, k in every:
        put(job, k).wait()


def choose(flag, operands, jobs):
    rows = operands[0].shape[0]
    anywhere = pl.BlockSpec(memory_space=pltpu.HBM)
    shapes = [(rows, job[3]) for job in jobs]
    return pl.pallas_call(
        functools.partial(choose_kernel, [job[:3] for job in jobs]),
        out_shape=[jax.ShapeDtypeStruct(shape, jnp.float32) for shape in shapes],
        in_specs=[pl.BlockSpec(memory_space=pltpu.SMEM)] + [anywhere] * len(operands),
        out_specs=[anywhere] * len(jobs),
        scratch_shapes=[pltpu.VMEM(shape, jnp.float32) for shape in shapes] + [pltpu.SemaphoreType.DMA((len(jobs), 3, 2))],
        compiler_params=pltpu.CompilerParams(vmem_limit_bytes=VMEM_BYTES),
        cost_estimate=pl.CostEstimate(flops=0, bytes_accessed=4 * operands[0].size, transcendentals=0),
        name="choose",
    )(flag, *operands)


def place_kernel(placed, ids_ref, *refs):
    received, out_ref, place_sem, stages = refs[: len(placed)], refs[len(placed) + 1], refs[len(placed) + 2], refs[len(placed) + 3 :]
    fetches, puts, at = [], [], 0
    for number, (from_ref, stage, (begin, size)) in enumerate(zip(received, stages, placed)):
        for index in range(from_ref.shape[0]):
            column = pl.multiple_of(ids_ref[at] * size + begin, 128)
            target = out_ref.at[:, pl.ds(column, from_ref.shape[-1])]
            fetches.append(pltpu.make_async_copy(from_ref.at[index], stage.at[index], place_sem.at[number, index, 0]))
            puts.append(pltpu.make_async_copy(stage.at[index], target, place_sem.at[number, index, 1]))
            at += 1
    for fetch in fetches:
        fetch.start()
    for fetch, put in zip(fetches, puts):
        fetch.wait()
        put.start()
    for put in puts:
        put.wait()


def place(out, received, ids):
    stacks = [stack for stack, _ in received]
    anywhere = pl.BlockSpec(memory_space=pltpu.HBM)
    return pl.pallas_call(
        functools.partial(place_kernel, [part for _, part in received]),
        out_shape=jax.ShapeDtypeStruct(out.shape, out.dtype),
        in_specs=[pl.BlockSpec(memory_space=pltpu.SMEM)] + [anywhere] * (len(stacks) + 1),
        out_specs=anywhere,
        scratch_shapes=[pltpu.SemaphoreType.DMA((len(stacks), max(v.shape[0] for v in stacks), 2))]
        + [pltpu.VMEM(v.shape, v.dtype) for v in stacks],
        input_output_aliases={len(stacks) + 1: 0},
        compiler_params=pltpu.CompilerParams(vmem_limit_bytes=VMEM_BYTES),
        cost_estimate=pl.CostEstimate(flops=0, bytes_accessed=8 * sum(v.size for v in stacks), transcendentals=0),
        name="place",
    )(ids, *stacks, out)


def gathered(loop, grp, jacobian):
    rows_here = jacobian.shape[1] // grp
    me, side = lax.axis_index("loop"), lax.axis_index("grp")
    both = lax.all_gather(jacobian, "grp")
    everything = lax.all_gather(both, "loop")
    mine = lax.dynamic_slice_in_dim(both, side * rows_here, rows_here, axis=2)
    left = left_operand(mine[0], mine[1])
    out = None
    for turn in range(loop):
        panel = (me + turn) % loop
        pair = tuple((lax.dynamic_index_in_dim(everything, panel, keepdims=False)[g],) for g in range(2))
        ids = jnp.stack([panel, side * rows_here]).astype(jnp.int32)
        out = panels(out, left, rows_here, jacobian.shape[1] * loop, [pair], ids, diagonal=None if turn else 0)
    return out


def rounds(loop, grp, jacobian):
    width = jacobian.shape[1]
    rows_here, columns = width // grp, width * loop
    me, side = lax.axis_index("loop"), lax.axis_index("grp")
    z, y, core = me // 4, (me // 2) % 2, me % 2

    along_x = lambda v: lax.ppermute(v, "grp", [(0, 1), (1, 0)])
    along_y = lambda v: lax.ppermute(v, "loop", [(i, i ^ 2) for i in range(16)])
    pair_z = lambda v: lax.ppermute(v, "loop", [(i, i ^ 4) for i in range(16)])
    inner = [(i, i + 4) for i in range(4, 8)] + [(i + 4, i) for i in range(4, 8)]
    mid_z = lambda v: lax.ppermute(v, "loop", inner)
    mid_z_all = lambda v: lax.ppermute(v, "loop", inner + [(i, i ^ 1) for i in (0, 1, 2, 3, 12, 13, 14, 15)])
    swap = lambda v: lax.ppermute(v, "loop", [(i, i ^ 1) for i in range(16)])
    together = lax.optimization_barrier
    after = lambda value, *first: together((value, first))[0]

    mate_z = z ^ 1
    near_z = jnp.where(z < 2, 2, 1)
    far_z = jnp.where(z < 2, 3, 0)
    shift = side * rows_here
    places = [(z, y), (z, 1 - y), (near_z, y), (mate_z, 1 - y), (mate_z, y), (near_z, 1 - y), (far_z, y), (far_z, 1 - y)]
    own = [zz * 4 + yy * 2 + core for zz, yy in places]
    other = [zz * 4 + yy * 2 + 1 - core for zz, yy in places]
    number = lambda *numbers: jnp.stack([jnp.int32(n) for n in numbers])
    outer = jnp.int32((z == 0) | (z == 3))
    ids = tuple(
        number(*n)
        for n in (
            own[:2] + [shift],
            own[2:4],
            own[4:6],
            own[6:] + other[2:4] + [outer],
            own[6:] + other[4:6] + [outer],
        )
    )
    put = number(*other[:2]), number(*other[6:])
    outer = number(outer)
    step = lambda out, left, turn, pairs, **kw: panels(out, left, rows_here, columns, pairs, ids[turn], **kw)
    whole, cut = (0, width), width * 5 // 8

    c = jacobian
    x_self, mid0, c_mate, y_self = along_x(c), mid_z(c), pair_z(c), along_y(c)
    own_columns = lambda v: lax.dynamic_slice_in_dim(v, shift, rows_here, axis=1)
    own_c = own_columns(c)
    own_c_o = swap(own_c)
    mid0, own_c, own_c_o, ids, put, outer = together((mid0, own_c, own_c_o, ids, put, outer))

    pair1 = pair_z(after(mid0, c_mate))
    mid1 = mid_z(c_mate)
    y_mate = along_y(after(c_mate, y_self))
    d_self = along_x(after(y_self, x_self))
    own_x = own_columns(x_self)
    left = left_operand(own_c, own_x, own_c_o, swap(own_x))

    (c_near,) = choose(outer, (after(pair1, left), mid0), [(0, 1, 0, width)])
    d_mate = pair_z(after(d_self, pair1, left))
    y_near = along_y(after(c_near, y_mate))
    x_near = along_x(after(c_near, d_self))
    out, send2 = step(None, left, 0, [((c,), (x_self,)), ((y_self,), (d_self,))], diagonal=0, sends=True)

    mid3 = mid_z_all(after(d_mate, out))
    pair3 = pair_z(after(mid1, d_mate, out))
    d_near = along_y(after(x_near, y_near))
    x_mate = along_x(after(c_mate, x_near))
    out, send3 = step(out, left, 1, [((c_near,), (x_near,)), ((y_mate,), (d_mate,))], sends=True)
    out = place(out, ((swap(send2), whole),), put[0])

    rest = width - cut
    early_c, early_3, late_c, late_3 = choose(
        outer,
        (after(pair3, out), mid1, mid3),
        [(0, 1, 0, cut), (2, 2, 0, cut), (0, 1, cut, rest), (2, 2, cut, rest)],
    )
    x_early = along_x(after(early_c, x_mate))
    d_early = pair_z(early_3)
    y_early = along_y(after(early_c, d_near))
    out, send4 = step(out, left, 2, [((c_mate,), (x_mate,)), ((y_near,), (d_near,))], sends=True)
    x_early, y_early, d_early, out = together((x_early, y_early, d_early, out))

    x_late = along_x(after(late_c, x_early))
    d_late = pair_z(after(late_3, d_early))
    y_late = along_y(after(late_c, y_early))
    pairs = [((early_c,), (x_early,)), ((y_early,), (d_early, early_3))]
    out, send5 = step(out, left, 3, pairs, received=((swap(send3), whole),), part=whole, sends=True)
    x_late, y_late, d_late, out = together((x_late, y_late, d_late, out))

    pairs = [((late_c,), (x_late,)), ((y_late,), (d_late, late_3))]
    out, send6 = step(out, left, 4, pairs, received=((swap(send4), whole),), part=(cut, width), sends=True)
    out = place(out, ((swap(send5), whole),), put[1])
    return place(out, ((swap(send6), (cut, width)),), put[1])


def solution(mesh):
    loop, grp = mesh.shape["loop"], mesh.shape["grp"]
    plan = rounds if (loop, grp) == (16, 2) else gathered
    return jax.shard_map(
        functools.partial(plan, loop, grp),
        mesh=mesh,
        in_specs=(P("grp", "loop"),),
        out_specs=P(("loop", "grp"), None),
        check_vma=False,
    )
```

```python
import functools

import jax
import jax.numpy as jnp
from jax import lax
from jax.experimental import pallas as pl
from jax.experimental.pallas import tpu as pltpu
from jax.sharding import PartitionSpec as P

damping = 0.1
VMEM_BYTES = 63 * 1024 * 1024 + 512 * 1024
COST = 1024


def split_high_low(value):
    high = value.astype(jnp.bfloat16)
    low = (value - high.astype(jnp.float32)).astype(jnp.bfloat16)
    return high, low


def left_kernel(*refs):
    left_ref = refs[-1]
    depth, rows = refs[0].shape
    for block in range(len(refs) // 2):
        for place, ref in enumerate(refs[2 * block : 2 * block + 2]):
            high, low = split_high_low(ref[...].T)
            for part, piece in enumerate((high, low)):
                target = pl.ds(rows * block, rows), pl.ds(2 * depth * part + depth * place, depth)
                left_ref[target] = piece


def left_operand(*halves):
    depth, rows = halves[0].shape
    shape = rows * (len(halves) // 2), 4 * depth
    return pl.pallas_call(
        left_kernel,
        out_shape=jax.ShapeDtypeStruct(shape, jnp.bfloat16),
        compiler_params=pltpu.CompilerParams(vmem_limit_bytes=VMEM_BYTES),
        cost_estimate=pl.CostEstimate(flops=COST, bytes_accessed=COST, transcendentals=0),
        name="left_operand",
    )(*halves)


def panel_kernel(sizes, diagonal, part, placed, width, tile, sends, ids_ref, left_hbm, *refs):
    count = sum(map(sum, sizes))
    blocks, received = refs[:count], refs[count : count + len(placed)]
    left_ref, held, done, left_sem, load_sem, store_sem, place_sem = refs[-7 - len(placed) : len(refs) - len(placed)]
    stages = refs[len(refs) - len(placed) :]
    out_ref, send_ref = refs[-9 - len(placed) : -7 - len(placed)] if sends else (refs[-8 - len(placed)], None)
    rows, (first, whole) = out_ref.shape[0], part
    tiles, panel_count = width // tile, len(sizes)
    turns = panel_count * tiles
    most = max(map(sum, sizes))
    height, depth = done.shape[1], left_ref.shape[1] // 2
    left = [left_ref.at[:, pl.ds(k * depth, depth)] for k in range(2)]
    left_copies = [
        pltpu.make_async_copy(left_hbm.at[pl.ds(0, height), pl.ds(k * depth, depth)], left[k], left_sem.at[k])
        for k in range(2)
    ]

    loads, at = [], 0
    for index, counts in enumerate(sizes):
        loads.append([[] for _ in range(tiles)])
        for place in range(sum(counts)):
            skip = first if blocks[at].shape[1] > width else 0
            for t in range(tiles):
                source = blocks[at].at[:, pl.ds(skip + t * tile, tile)]
                target = held.at[index % 2, place, :, pl.ds(t * tile, tile)]
                loads[index][t].append(pltpu.make_async_copy(source, target, load_sem.at[index % 2, place, t]))
            at += 1
    fetches, puts, at = [], [], panel_count
    for number, (from_ref, stage, (begin, size)) in enumerate(zip(received, stages, placed)):
        for index in range(from_ref.shape[0]):
            column = pl.multiple_of(ids_ref[at] * size + begin, 128)
            target = out_ref.at[:, pl.ds(column, from_ref.shape[-1])]
            fetches.append(pltpu.make_async_copy(from_ref.at[index], stage.at[index], place_sem.at[number, index, 0]))
            puts.append(pltpu.make_async_copy(stage.at[index], target, place_sem.at[number, index, 1]))
            at += 1

    def stores(turn):
        index, column = turn // tiles, pl.multiple_of(lax.rem(turn, tiles) * tile, 128)
        slot = lax.rem(turn, 2)
        place = pl.multiple_of(ids_ref[index] * whole + first + column, 128)
        copies = [(done.at[slot, pl.ds(0, rows)], out_ref.at[:, pl.ds(place, tile)], store_sem.at[slot, 0])]
        if sends:
            target = send_ref.at[index, :, pl.ds(column, tile)]
            copies.append((done.at[slot, pl.ds(rows, rows)], target, store_sem.at[slot, 1]))
        return [pltpu.make_async_copy(*copy) for copy in copies]

    def start(copies):
        for copy in copies:
            copy.start()

    def wait(copies):
        for copy in copies:
            copy.wait()

    start(loads[0][0] + left_copies)
    for copies in loads[0][1:]:
        start(copies)
    left_copies[0].wait()
    if tile != 512:
        left_copies[1].wait()

    def turn_body(turn, carry):
        index, column = turn // tiles, pl.multiple_of(lax.rem(turn, tiles) * tile, 128)
        slot = lax.rem(index, 2)
        for here in range(turns):

            @pl.when(turn == here)
            def arrive(here=here):
                wait(loads[here // tiles][here % tiles])
                if here == 0:
                    for copies in loads[1] if panel_count > 1 else []:
                        start(copies)
                    start(fetches)

        @pl.when(turn >= 2)
        def free():
            wait(stores(turn - 2))

        @pl.when(turn == turns // 2)
        def put():
            wait(fetches)
            start(puts)

        block = [held[slot, k, :, pl.ds(column, tile)] for k in range(most)]
        if most > 2:
            extra = functools.reduce(jnp.logical_or, [index == i for i, n in enumerate(sizes) if sum(n) > 2])
            block[1] = jnp.where(extra & (ids_ref[ids_ref.shape[0] - 1] == 0), block[2], block[1])
        halves = [split_high_low(value) for value in block[:2]]
        high, low = (jnp.concatenate(pieces, axis=0) for pieces in zip(*halves))
        dot = functools.partial(jnp.dot, preferred_element_type=jnp.float32)
        product = dot(left[0][...], high) + dot(left[0][...], low)
        if tile == 512:

            @pl.when(turn == 0)
            def rest_of_left():
                left_copies[1].wait()

        product += dot(left[1][...], high)
        if diagonal is not None:
            row_ids = lax.broadcasted_iota(jnp.int32, product.shape, 0) + ids_ref[ids_ref.shape[0] - 1]
            col_ids = lax.broadcasted_iota(jnp.int32, product.shape, 1) + column
            own = lax.broadcasted_iota(jnp.int32, product.shape, 0) < rows
            hit = (row_ids == col_ids) & own & (index == diagonal)
            product = jnp.where(hit, product * jnp.float32(1.0 + damping), product)
        done[lax.rem(turn, 2)] = product
        start(stores(turn))
        for here in range(panel_count - 2):

            @pl.when(turn == here * tiles + tiles - 1)
            def fetch(later=loads[here + 2]):
                for copies in later:
                    start(copies)

        return carry

    lax.fori_loop(0, turns, turn_body, 0)
    for turn in range(max(0, turns - 2), turns):
        wait(stores(turn))
    wait(puts)


def panels(out, left, rows, columns, pairs, ids, received=(), diagonal=None, part=None, width=None, sends=False):
    depth, width = pairs[0][0][0].shape[0], width or pairs[0][0][0].shape[1]
    sizes = tuple(tuple(len(half) for half in pair) for pair in pairs)
    args = [ids, left] + [array for pair in pairs for half in pair for array in half]
    args += [stack for stack, _ in received]
    aliases = {}
    if out is not None:
        aliases = {len(args): 0}
        args.append(out)
    anywhere = pl.BlockSpec(memory_space=pl.ANY)
    most = max(map(sum, sizes))
    tile = 512 if width % 512 == 0 else 256 if width % 256 == 0 else width
    height = 2 * rows if sends else rows
    shapes = [jax.ShapeDtypeStruct((rows, columns), jnp.float32)]
    if sends:
        shapes.append(jax.ShapeDtypeStruct((len(pairs), rows, width), jnp.float32))
    stacked = max([stack.shape[0] for stack, _ in received], default=1)
    outs = pl.pallas_call(
        functools.partial(
            panel_kernel,
            sizes,
            diagonal,
            part or (0, width),
            tuple(place for _, place in received),
            width,
            tile,
            sends,
        ),
        out_shape=shapes,
        in_specs=[pl.BlockSpec(memory_space=pltpu.SMEM)] + [anywhere] * (len(args) - 1),
        out_specs=[anywhere] * len(shapes),
        scratch_shapes=[
            pltpu.VMEM((height, left.shape[1]), left.dtype),
            pltpu.VMEM((2, most, depth, width), jnp.float32),
            pltpu.VMEM((2, height, tile), jnp.float32),
            pltpu.SemaphoreType.DMA((2,)),
            pltpu.SemaphoreType.DMA((2, most, width // tile)),
            pltpu.SemaphoreType.DMA((2, 2)),
            pltpu.SemaphoreType.DMA((max(1, len(received)), stacked, 2)),
            *[pltpu.VMEM(stack.shape, jnp.float32) for stack, _ in received],
        ],
        input_output_aliases=aliases,
        compiler_params=pltpu.CompilerParams(vmem_limit_bytes=VMEM_BYTES),
        cost_estimate=pl.CostEstimate(
            flops=30 * height * left.shape[1] * width * len(pairs),
            bytes_accessed=4 * width * len(pairs) * (height + 2 * depth),
            transcendentals=0,
        ),
        name="panels",
    )(*args)
    return outs if sends else outs[0]


def choose_kernel(jobs, flag_ref, *refs):
    outs = refs[-1 - 2 * len(jobs) : -1 - len(jobs)]
    stages, sems = refs[-1 - len(jobs) : -1], refs[-1]
    pieces = sems.shape[1]
    rows = [pl.ds(k * (stages[0].shape[0] // pieces), stages[0].shape[0] // pieces) for k in range(pieces)]

    def fetch(job, k, pick):
        first, columns = jobs[job], pl.ds(jobs[job][2], stages[job].shape[1])
        return pltpu.make_async_copy(refs[first[pick]].at[rows[k], columns], stages[job].at[rows[k]], sems.at[job, k, 0])

    def put(job, k):
        return pltpu.make_async_copy(stages[job].at[rows[k]], outs[job].at[rows[k]], sems.at[job, k, 1])

    every = [(job, k) for job in range(len(jobs)) for k in range(pieces)]
    for pick in range(2):

        @pl.when(flag_ref[0] == 1 - pick)
        def start(pick=pick):
            for job, k in every:
                fetch(job, k, pick).start()

    for job, k in every:
        fetch(job, k, 0).wait()
        put(job, k).start()
    for job, k in every:
        put(job, k).wait()


def choose(flag, operands, jobs):
    rows = operands[0].shape[0]
    anywhere = pl.BlockSpec(memory_space=pltpu.HBM)
    shapes = [(rows, job[3]) for job in jobs]
    return pl.pallas_call(
        functools.partial(choose_kernel, [job[:3] for job in jobs]),
        out_shape=[jax.ShapeDtypeStruct(shape, jnp.float32) for shape in shapes],
        in_specs=[pl.BlockSpec(memory_space=pltpu.SMEM)] + [anywhere] * len(operands),
        out_specs=[anywhere] * len(jobs),
        scratch_shapes=[pltpu.VMEM(shape, jnp.float32) for shape in shapes] + [pltpu.SemaphoreType.DMA((len(jobs), 3, 2))],
        compiler_params=pltpu.CompilerParams(vmem_limit_bytes=VMEM_BYTES),
        cost_estimate=pl.CostEstimate(flops=0, bytes_accessed=4 * operands[0].size, transcendentals=0),
        name="choose",
    )(flag, *operands)


def place_kernel(placed, ids_ref, *refs):
    received, out_ref, place_sem, stages = refs[: len(placed)], refs[len(placed) + 1], refs[len(placed) + 2], refs[len(placed) + 3 :]
    fetches, puts, at = [], [], 0
    for number, (from_ref, stage, (begin, size)) in enumerate(zip(received, stages, placed)):
        for index in range(from_ref.shape[0]):
            column = pl.multiple_of(ids_ref[at] * size + begin, 128)
            target = out_ref.at[:, pl.ds(column, from_ref.shape[-1])]
            fetches.append(pltpu.make_async_copy(from_ref.at[index], stage.at[index], place_sem.at[number, index, 0]))
            puts.append(pltpu.make_async_copy(stage.at[index], target, place_sem.at[number, index, 1]))
            at += 1
    for fetch in fetches:
        fetch.start()
    for fetch, put in zip(fetches, puts):
        fetch.wait()
        put.start()
    for put in puts:
        put.wait()


def place(out, received, ids):
    stacks = [stack for stack, _ in received]
    anywhere = pl.BlockSpec(memory_space=pltpu.HBM)
    return pl.pallas_call(
        functools.partial(place_kernel, [part for _, part in received]),
        out_shape=jax.ShapeDtypeStruct(out.shape, out.dtype),
        in_specs=[pl.BlockSpec(memory_space=pltpu.SMEM)] + [anywhere] * (len(stacks) + 1),
        out_specs=anywhere,
        scratch_shapes=[pltpu.SemaphoreType.DMA((len(stacks), max(v.shape[0] for v in stacks), 2))]
        + [pltpu.VMEM(v.shape, v.dtype) for v in stacks],
        input_output_aliases={len(stacks) + 1: 0},
        compiler_params=pltpu.CompilerParams(vmem_limit_bytes=VMEM_BYTES),
        cost_estimate=pl.CostEstimate(flops=0, bytes_accessed=8 * sum(v.size for v in stacks), transcendentals=0),
        name="place",
    )(ids, *stacks, out)


def gathered(loop, grp, jacobian):
    rows_here = jacobian.shape[1] // grp
    me, side = lax.axis_index("loop"), lax.axis_index("grp")
    both = lax.all_gather(jacobian, "grp")
    everything = lax.all_gather(both, "loop")
    mine = lax.dynamic_slice_in_dim(both, side * rows_here, rows_here, axis=2)
    left = left_operand(mine[0], mine[1])
    out = None
    for turn in range(loop):
        panel = (me + turn) % loop
        pair = tuple((lax.dynamic_index_in_dim(everything, panel, keepdims=False)[g],) for g in range(2))
        ids = jnp.stack([panel, side * rows_here]).astype(jnp.int32)
        out = panels(out, left, rows_here, jacobian.shape[1] * loop, [pair], ids, diagonal=None if turn else 0)
    return out


def rounds(loop, grp, jacobian):
    width = jacobian.shape[1]
    rows_here, columns = width // grp, width * loop
    me, side = lax.axis_index("loop"), lax.axis_index("grp")
    z, y, core = me // 4, (me // 2) % 2, me % 2

    along_x = lambda v: lax.ppermute(v, "grp", [(0, 1), (1, 0)])
    along_y = lambda v: lax.ppermute(v, "loop", [(i, i ^ 2) for i in range(16)])
    pair_z = lambda v: lax.ppermute(v, "loop", [(i, i ^ 4) for i in range(16)])
    inner = [(i, i + 4) for i in range(4, 8)] + [(i + 4, i) for i in range(4, 8)]
    mid_z = lambda v: lax.ppermute(v, "loop", inner)
    mid_z_all = lambda v: lax.ppermute(v, "loop", inner + [(i, i ^ 1) for i in (0, 1, 2, 3, 12, 13, 14, 15)])
    swap = lambda v: lax.ppermute(v, "loop", [(i, i ^ 1) for i in range(16)])
    together = lax.optimization_barrier
    after = lambda value, *first: together((value, first))[0]

    mate_z = z ^ 1
    near_z = jnp.where(z < 2, 2, 1)
    far_z = jnp.where(z < 2, 3, 0)
    shift = side * rows_here
    places = [(z, y), (z, 1 - y), (near_z, y), (mate_z, 1 - y), (mate_z, y), (near_z, 1 - y), (far_z, y), (far_z, 1 - y)]
    own = [zz * 4 + yy * 2 + core for zz, yy in places]
    other = [zz * 4 + yy * 2 + 1 - core for zz, yy in places]
    number = lambda *numbers: jnp.stack([jnp.int32(n) for n in numbers])
    outer = jnp.int32((z == 0) | (z == 3))
    ids = tuple(
        number(*n)
        for n in (
            own[:2] + [shift],
            own[2:4],
            own[4:6],
            own[6:] + other[2:4] + [outer],
            own[6:] + other[4:6] + [outer],
        )
    )
    put = number(*other[:2]), number(*other[6:])
    outer = number(outer)
    step = lambda out, left, turn, pairs, **kw: panels(out, left, rows_here, columns, pairs, ids[turn], **kw)
    whole, cut = (0, width), width * 5 // 8

    c = jacobian
    x_self, mid0, c_mate, y_self = along_x(c), mid_z(c), pair_z(c), along_y(c)
    own_columns = lambda v: lax.dynamic_slice_in_dim(v, shift, rows_here, axis=1)
    own_c = own_columns(c)
    own_c_o = swap(own_c)
    mid0, own_c, own_c_o, ids, put, outer = together((mid0, own_c, own_c_o, ids, put, outer))

    pair1 = pair_z(mid0)
    mid1 = mid_z(c_mate)
    y_mate = along_y(after(c_mate, y_self))
    d_self = along_x(after(y_self, x_self))
    own_x = own_columns(x_self)
    left = left_operand(own_c, own_x, own_c_o, swap(own_x))

    (c_near,) = choose(outer, (after(pair1, left), mid0), [(0, 1, 0, width)])
    d_mate = pair_z(after(d_self, pair1, left))
    y_near = along_y(after(c_near, y_mate))
    x_near = along_x(after(c_near, d_self))
    out, send2 = step(None, left, 0, [((c,), (x_self,)), ((y_self,), (d_self,))], diagonal=0, sends=True)

    mid3 = mid_z_all(after(d_mate, out))
    pair3 = pair_z(after(mid1, out))
    d_near = along_y(after(x_near, y_near))
    x_mate = along_x(after(c_mate, x_near))
    out, send3 = step(out, left, 1, [((c_near,), (x_near,)), ((y_mate,), (d_mate,))], sends=True)
    out = place(out, ((swap(send2), whole),), put[0])

    rest = width - cut
    early_c, early_3, late_c, late_3 = choose(
        outer,
        (after(pair3, out), mid1, mid3),
        [(0, 1, 0, cut), (2, 2, 0, cut), (0, 1, cut, rest), (2, 2, cut, rest)],
    )
    x_early = along_x(after(early_c, x_mate))
    d_early = pair_z(early_3)
    y_early = along_y(after(early_c, d_near))
    out, send4 = step(out, left, 2, [((c_mate,), (x_mate,)), ((y_near,), (d_near,))], sends=True)
    x_early, y_early, d_early, out = together((x_early, y_early, d_early, out))

    x_late = along_x(after(late_c, x_early))
    d_late = pair_z(after(late_3, d_early))
    y_late = along_y(after(late_c, y_early))
    pairs = [((early_c,), (x_early,)), ((y_early,), (d_early, early_3))]
    out, send5 = step(out, left, 3, pairs, received=((swap(send3), whole),), part=whole, sends=True)
    x_late, y_late, d_late, out = together((x_late, y_late, d_late, out))

    pairs = [((late_c,), (x_late,)), ((y_late,), (d_late, late_3))]
    out, send6 = step(out, left, 4, pairs, received=((swap(send4), whole),), part=(cut, width), sends=True)
    out = place(out, ((swap(send5), whole),), put[1])
    return place(out, ((swap(send6), (cut, width)),), put[1])


def solution(mesh):
    loop, grp = mesh.shape["loop"], mesh.shape["grp"]
    plan = rounds if (loop, grp) == (16, 2) else gathered
    return jax.shard_map(
        functools.partial(plan, loop, grp),
        mesh=mesh,
        in_specs=(P("grp", "loop"),),
        out_specs=P(("loop", "grp"), None),
        check_vma=False,
    )
```

```python
import functools

import jax
import jax.numpy as jnp
from jax import lax
from jax.experimental import pallas as pl
from jax.experimental.pallas import tpu as pltpu
from jax.sharding import PartitionSpec as P

damping = 0.1
VMEM_BYTES = 63 * 1024 * 1024 + 512 * 1024
COST = 1024


def split_high_low(value):
    high = value.astype(jnp.bfloat16)
    low = (value - high.astype(jnp.float32)).astype(jnp.bfloat16)
    return high, low


def left_kernel(*refs):
    left_ref = refs[-1]
    depth, rows = refs[0].shape
    for block in range(len(refs) // 2):
        for place, ref in enumerate(refs[2 * block : 2 * block + 2]):
            high, low = split_high_low(ref[...].T)
            for part, piece in enumerate((high, low)):
                target = pl.ds(rows * block, rows), pl.ds(2 * depth * part + depth * place, depth)
                left_ref[target] = piece


def left_operand(*halves):
    depth, rows = halves[0].shape
    shape = rows * (len(halves) // 2), 4 * depth
    return pl.pallas_call(
        left_kernel,
        out_shape=jax.ShapeDtypeStruct(shape, jnp.bfloat16),
        compiler_params=pltpu.CompilerParams(vmem_limit_bytes=VMEM_BYTES),
        cost_estimate=pl.CostEstimate(flops=COST, bytes_accessed=COST, transcendentals=0),
        name="left_operand",
    )(*halves)


def panel_kernel(sizes, diagonal, part, placed, width, tile, sends, ids_ref, left_hbm, *refs):
    count = sum(map(sum, sizes))
    blocks, received = refs[:count], refs[count : count + len(placed)]
    left_ref, held, done, left_sem, load_sem, store_sem, place_sem = refs[-7 - len(placed) : len(refs) - len(placed)]
    stages = refs[len(refs) - len(placed) :]
    out_ref, send_ref = refs[-9 - len(placed) : -7 - len(placed)] if sends else (refs[-8 - len(placed)], None)
    rows, (first, whole) = out_ref.shape[0], part
    tiles, panel_count = width // tile, len(sizes)
    turns = panel_count * tiles
    most = max(map(sum, sizes))
    height, depth = done.shape[1], left_ref.shape[1] // 2
    left = [left_ref.at[:, pl.ds(k * depth, depth)] for k in range(2)]
    left_copies = [
        pltpu.make_async_copy(left_hbm.at[pl.ds(0, height), pl.ds(k * depth, depth)], left[k], left_sem.at[k])
        for k in range(2)
    ]

    loads, at = [], 0
    for index, counts in enumerate(sizes):
        loads.append([[] for _ in range(tiles)])
        for place in range(sum(counts)):
            skip = first if blocks[at].shape[1] > width else 0
            for t in range(tiles):
                source = blocks[at].at[:, pl.ds(skip + t * tile, tile)]
                target = held.at[index % 2, place, :, pl.ds(t * tile, tile)]
                loads[index][t].append(pltpu.make_async_copy(source, target, load_sem.at[index % 2, place, t]))
            at += 1
    fetches, puts, at = [], [], panel_count
    for number, (from_ref, stage, (begin, size)) in enumerate(zip(received, stages, placed)):
        for index in range(from_ref.shape[0]):
            column = pl.multiple_of(ids_ref[at] * size + begin, 128)
            target = out_ref.at[:, pl.ds(column, from_ref.shape[-1])]
            fetches.append(pltpu.make_async_copy(from_ref.at[index], stage.at[index], place_sem.at[number, index, 0]))
            puts.append(pltpu.make_async_copy(stage.at[index], target, place_sem.at[number, index, 1]))
            at += 1

    def stores(turn):
        index, column = turn // tiles, pl.multiple_of(lax.rem(turn, tiles) * tile, 128)
        slot = lax.rem(turn, 2)
        place = pl.multiple_of(ids_ref[index] * whole + first + column, 128)
        copies = [(done.at[slot, pl.ds(0, rows)], out_ref.at[:, pl.ds(place, tile)], store_sem.at[slot, 0])]
        if sends:
            target = send_ref.at[index, :, pl.ds(column, tile)]
            copies.append((done.at[slot, pl.ds(rows, rows)], target, store_sem.at[slot, 1]))
        return [pltpu.make_async_copy(*copy) for copy in copies]

    def start(copies):
        for copy in copies:
            copy.start()

    def wait(copies):
        for copy in copies:
            copy.wait()

    start(loads[0][0] + left_copies)
    for copies in loads[0][1:]:
        start(copies)
    left_copies[0].wait()
    if tile != 512:
        left_copies[1].wait()

    def turn_body(turn, carry):
        index, column = turn // tiles, pl.multiple_of(lax.rem(turn, tiles) * tile, 128)
        slot = lax.rem(index, 2)
        for here in range(turns):

            @pl.when(turn == here)
            def arrive(here=here):
                wait(loads[here // tiles][here % tiles])
                if here == 0:
                    for copies in loads[1] if panel_count > 1 else []:
                        start(copies)
                    start(fetches)

        @pl.when(turn >= 2)
        def free():
            wait(stores(turn - 2))

        @pl.when(turn == turns // 2)
        def put():
            wait(fetches)
            start(puts)

        block = [held[slot, k, :, pl.ds(column, tile)] for k in range(most)]
        if most > 2:
            extra = functools.reduce(jnp.logical_or, [index == i for i, n in enumerate(sizes) if sum(n) > 2])
            block[1] = jnp.where(extra & (ids_ref[ids_ref.shape[0] - 1] == 0), block[2], block[1])
        halves = [split_high_low(value) for value in block[:2]]
        high, low = (jnp.concatenate(pieces, axis=0) for pieces in zip(*halves))
        dot = functools.partial(jnp.dot, preferred_element_type=jnp.float32)
        if tile == 512:
            product = dot(left[0][...], high) + dot(left[0][...], low)

            @pl.when(turn == 0)
            def rest_of_left():
                left_copies[1].wait()

            product += dot(left[1][...], high)
        else:
            product = dot(left[0][...], high) + dot(left_ref[...], jnp.concatenate([low, high], axis=0))
        if diagonal is not None:
            row_ids = lax.broadcasted_iota(jnp.int32, product.shape, 0) + ids_ref[ids_ref.shape[0] - 1]
            col_ids = lax.broadcasted_iota(jnp.int32, product.shape, 1) + column
            own = lax.broadcasted_iota(jnp.int32, product.shape, 0) < rows
            hit = (row_ids == col_ids) & own & (index == diagonal)
            product = jnp.where(hit, product * jnp.float32(1.0 + damping), product)
        done[lax.rem(turn, 2)] = product
        start(stores(turn))
        for here in range(panel_count - 2):

            @pl.when(turn == here * tiles + tiles - 1)
            def fetch(later=loads[here + 2]):
                for copies in later:
                    start(copies)

        return carry

    lax.fori_loop(0, turns, turn_body, 0)
    for turn in range(max(0, turns - 2), turns):
        wait(stores(turn))
    wait(puts)


def panels(out, left, rows, columns, pairs, ids, received=(), diagonal=None, part=None, width=None, sends=False):
    depth, width = pairs[0][0][0].shape[0], width or pairs[0][0][0].shape[1]
    sizes = tuple(tuple(len(half) for half in pair) for pair in pairs)
    args = [ids, left] + [array for pair in pairs for half in pair for array in half]
    args += [stack for stack, _ in received]
    aliases = {}
    if out is not None:
        aliases = {len(args): 0}
        args.append(out)
    anywhere = pl.BlockSpec(memory_space=pl.ANY)
    most = max(map(sum, sizes))
    tile = 512 if width % 512 == 0 else 256 if width % 256 == 0 else width
    height = 2 * rows if sends else rows
    shapes = [jax.ShapeDtypeStruct((rows, columns), jnp.float32)]
    if sends:
        shapes.append(jax.ShapeDtypeStruct((len(pairs), rows, width), jnp.float32))
    stacked = max([stack.shape[0] for stack, _ in received], default=1)
    outs = pl.pallas_call(
        functools.partial(
            panel_kernel,
            sizes,
            diagonal,
            part or (0, width),
            tuple(place for _, place in received),
            width,
            tile,
            sends,
        ),
        out_shape=shapes,
        in_specs=[pl.BlockSpec(memory_space=pltpu.SMEM)] + [anywhere] * (len(args) - 1),
        out_specs=[anywhere] * len(shapes),
        scratch_shapes=[
            pltpu.VMEM((height, left.shape[1]), left.dtype),
            pltpu.VMEM((2, most, depth, width), jnp.float32),
            pltpu.VMEM((2, height, tile), jnp.float32),
            pltpu.SemaphoreType.DMA((2,)),
            pltpu.SemaphoreType.DMA((2, most, width // tile)),
            pltpu.SemaphoreType.DMA((2, 2)),
            pltpu.SemaphoreType.DMA((max(1, len(received)), stacked, 2)),
            *[pltpu.VMEM(stack.shape, jnp.float32) for stack, _ in received],
        ],
        input_output_aliases=aliases,
        compiler_params=pltpu.CompilerParams(vmem_limit_bytes=VMEM_BYTES),
        cost_estimate=pl.CostEstimate(
            flops=30 * height * left.shape[1] * width * len(pairs),
            bytes_accessed=4 * width * len(pairs) * (height + 2 * depth),
            transcendentals=0,
        ),
        name="panels",
    )(*args)
    return outs if sends else outs[0]


def choose_kernel(jobs, flag_ref, *refs):
    outs = refs[-1 - 2 * len(jobs) : -1 - len(jobs)]
    stages, sems = refs[-1 - len(jobs) : -1], refs[-1]
    pieces = sems.shape[1]
    rows = [pl.ds(k * (stages[0].shape[0] // pieces), stages[0].shape[0] // pieces) for k in range(pieces)]

    def fetch(job, k, pick):
        first, columns = jobs[job], pl.ds(jobs[job][2], stages[job].shape[1])
        return pltpu.make_async_copy(refs[first[pick]].at[rows[k], columns], stages[job].at[rows[k]], sems.at[job, k, 0])

    def put(job, k):
        return pltpu.make_async_copy(stages[job].at[rows[k]], outs[job].at[rows[k]], sems.at[job, k, 1])

    every = [(job, k) for job in range(len(jobs)) for k in range(pieces)]
    for pick in range(2):

        @pl.when(flag_ref[0] == 1 - pick)
        def start(pick=pick):
            for job, k in every:
                fetch(job, k, pick).start()

    for job, k in every:
        fetch(job, k, 0).wait()
        put(job, k).start()
    for job, k in every:
        put(job, k).wait()


def choose(flag, operands, jobs):
    rows = operands[0].shape[0]
    anywhere = pl.BlockSpec(memory_space=pltpu.HBM)
    shapes = [(rows, job[3]) for job in jobs]
    return pl.pallas_call(
        functools.partial(choose_kernel, [job[:3] for job in jobs]),
        out_shape=[jax.ShapeDtypeStruct(shape, jnp.float32) for shape in shapes],
        in_specs=[pl.BlockSpec(memory_space=pltpu.SMEM)] + [anywhere] * len(operands),
        out_specs=[anywhere] * len(jobs),
        scratch_shapes=[pltpu.VMEM(shape, jnp.float32) for shape in shapes] + [pltpu.SemaphoreType.DMA((len(jobs), 3, 2))],
        compiler_params=pltpu.CompilerParams(vmem_limit_bytes=VMEM_BYTES),
        cost_estimate=pl.CostEstimate(flops=0, bytes_accessed=4 * operands[0].size, transcendentals=0),
        name="choose",
    )(flag, *operands)


def place_kernel(placed, ids_ref, *refs):
    received, out_ref, place_sem, stages = refs[: len(placed)], refs[len(placed) + 1], refs[len(placed) + 2], refs[len(placed) + 3 :]
    fetches, puts, at = [], [], 0
    for number, (from_ref, stage, (begin, size)) in enumerate(zip(received, stages, placed)):
        for index in range(from_ref.shape[0]):
            column = pl.multiple_of(ids_ref[at] * size + begin, 128)
            target = out_ref.at[:, pl.ds(column, from_ref.shape[-1])]
            fetches.append(pltpu.make_async_copy(from_ref.at[index], stage.at[index], place_sem.at[number, index, 0]))
            puts.append(pltpu.make_async_copy(stage.at[index], target, place_sem.at[number, index, 1]))
            at += 1
    for fetch in fetches:
        fetch.start()
    for fetch, put in zip(fetches, puts):
        fetch.wait()
        put.start()
    for put in puts:
        put.wait()


def place(out, received, ids):
    stacks = [stack for stack, _ in received]
    anywhere = pl.BlockSpec(memory_space=pltpu.HBM)
    return pl.pallas_call(
        functools.partial(place_kernel, [part for _, part in received]),
        out_shape=jax.ShapeDtypeStruct(out.shape, out.dtype),
        in_specs=[pl.BlockSpec(memory_space=pltpu.SMEM)] + [anywhere] * (len(stacks) + 1),
        out_specs=anywhere,
        scratch_shapes=[pltpu.SemaphoreType.DMA((len(stacks), max(v.shape[0] for v in stacks), 2))]
        + [pltpu.VMEM(v.shape, v.dtype) for v in stacks],
        input_output_aliases={len(stacks) + 1: 0},
        compiler_params=pltpu.CompilerParams(vmem_limit_bytes=VMEM_BYTES),
        cost_estimate=pl.CostEstimate(flops=0, bytes_accessed=8 * sum(v.size for v in stacks), transcendentals=0),
        name="place",
    )(ids, *stacks, out)


def gathered(loop, grp, jacobian):
    rows_here = jacobian.shape[1] // grp
    me, side = lax.axis_index("loop"), lax.axis_index("grp")
    both = lax.all_gather(jacobian, "grp")
    everything = lax.all_gather(both, "loop")
    mine = lax.dynamic_slice_in_dim(both, side * rows_here, rows_here, axis=2)
    left = left_operand(mine[0], mine[1])
    out = None
    for turn in range(loop):
        panel = (me + turn) % loop
        pair = tuple((lax.dynamic_index_in_dim(everything, panel, keepdims=False)[g],) for g in range(2))
        ids = jnp.stack([panel, side * rows_here]).astype(jnp.int32)
        out = panels(out, left, rows_here, jacobian.shape[1] * loop, [pair], ids, diagonal=None if turn else 0)
    return out


def rounds(loop, grp, jacobian):
    width = jacobian.shape[1]
    rows_here, columns = width // grp, width * loop
    me, side = lax.axis_index("loop"), lax.axis_index("grp")
    z, y, core = me // 4, (me // 2) % 2, me % 2

    along_x = lambda v: lax.ppermute(v, "grp", [(0, 1), (1, 0)])
    along_y = lambda v: lax.ppermute(v, "loop", [(i, i ^ 2) for i in range(16)])
    pair_z = lambda v: lax.ppermute(v, "loop", [(i, i ^ 4) for i in range(16)])
    inner = [(i, i + 4) for i in range(4, 8)] + [(i + 4, i) for i in range(4, 8)]
    mid_z = lambda v: lax.ppermute(v, "loop", inner)
    mid_z_all = lambda v: lax.ppermute(v, "loop", inner + [(i, i ^ 1) for i in (0, 1, 2, 3, 12, 13, 14, 15)])
    swap = lambda v: lax.ppermute(v, "loop", [(i, i ^ 1) for i in range(16)])
    together = lax.optimization_barrier
    after = lambda value, *first: together((value, first))[0]

    mate_z = z ^ 1
    near_z = jnp.where(z < 2, 2, 1)
    far_z = jnp.where(z < 2, 3, 0)
    shift = side * rows_here
    places = [(z, y), (z, 1 - y), (near_z, y), (mate_z, 1 - y), (mate_z, y), (near_z, 1 - y), (far_z, y), (far_z, 1 - y)]
    own = [zz * 4 + yy * 2 + core for zz, yy in places]
    other = [zz * 4 + yy * 2 + 1 - core for zz, yy in places]
    number = lambda *numbers: jnp.stack([jnp.int32(n) for n in numbers])
    outer = jnp.int32((z == 0) | (z == 3))
    ids = tuple(
        number(*n)
        for n in (
            own[:2] + [shift],
            own[2:4],
            own[4:6],
            own[6:] + other[2:4] + [outer],
            own[6:] + other[4:6] + [outer],
        )
    )
    put = number(*other[:2]), number(*other[6:])
    outer = number(outer)
    step = lambda out, left, turn, pairs, **kw: panels(out, left, rows_here, columns, pairs, ids[turn], **kw)
    whole, cut = (0, width), width * 5 // 8

    c = jacobian
    x_self, mid0, c_mate, y_self = along_x(c), mid_z(c), pair_z(c), along_y(c)
    own_columns = lambda v: lax.dynamic_slice_in_dim(v, shift, rows_here, axis=1)
    own_c = own_columns(c)
    own_c_o = swap(own_c)
    mid0, own_c, own_c_o, ids, put, outer = together((mid0, own_c, own_c_o, ids, put, outer))

    pair1 = pair_z(mid0)
    mid1 = mid_z(c_mate)
    y_mate = along_y(after(c_mate, y_self))
    d_self = along_x(after(y_self, x_self))
    own_x = own_columns(x_self)
    left = left_operand(own_c, own_x, own_c_o, swap(own_x))

    (c_near,) = choose(outer, (after(pair1, left), mid0), [(0, 1, 0, width)])
    d_mate = pair_z(after(d_self, pair1, left))
    y_near = along_y(after(c_near, y_mate))
    x_near = along_x(after(c_near, d_self))
    out, send2 = step(None, left, 0, [((c,), (x_self,)), ((y_self,), (d_self,))], diagonal=0, sends=True)

    mid3 = mid_z_all(after(d_mate, out))
    pair3 = pair_z(after(mid1, out))
    d_near = along_y(after(x_near, y_near))
    x_mate = along_x(after(c_mate, x_near))
    out, send3 = step(out, left, 1, [((c_near,), (x_near,)), ((y_mate,), (d_mate,))], sends=True)
    out = place(out, ((swap(send2), whole),), put[0])

    rest = width - cut
    early_c, early_3, late_c, late_3 = choose(
        outer,
        (after(pair3, out), mid1, mid3),
        [(0, 1, 0, cut), (2, 2, 0, cut), (0, 1, cut, rest), (2, 2, cut, rest)],
    )
    x_early = along_x(after(early_c, x_mate))
    d_early = pair_z(early_3)
    y_early = along_y(after(early_c, d_near))
    out, send4 = step(out, left, 2, [((c_mate,), (x_mate,)), ((y_near,), (d_near,))], sends=True)
    x_early, y_early, d_early, out = together((x_early, y_early, d_early, out))

    x_late = along_x(after(late_c, x_early))
    d_late = pair_z(after(late_3, d_early))
    y_late = along_y(after(late_c, y_early))
    pairs = [((early_c,), (x_early,)), ((y_early,), (d_early, early_3))]
    out, send5 = step(out, left, 3, pairs, received=((swap(send3), whole),), part=whole, sends=True)
    x_late, y_late, d_late, out = together((x_late, y_late, d_late, out))

    pairs = [((late_c,), (x_late,)), ((y_late,), (d_late, late_3))]
    out, send6 = step(out, left, 4, pairs, received=((swap(send4), whole),), part=(cut, width), sends=True)
    out = place(out, ((swap(send5), whole),), put[1])
    return place(out, ((swap(send6), (cut, width)),), put[1])


def solution(mesh):
    loop, grp = mesh.shape["loop"], mesh.shape["grp"]
    plan = rounds if (loop, grp) == (16, 2) else gathered
    return jax.shard_map(
        functools.partial(plan, loop, grp),
        mesh=mesh,
        in_specs=(P("grp", "loop"),),
        out_specs=P(("loop", "grp"), None),
        check_vma=False,
    )
```
